256 devices in a mesh: gy: 32 (over x, y, core), gz: 8 (over z).
Axes of the slice: x: 4, y: 4, z: 8, core: 2. Of those that a mesh axis runs over, the one named last changes fastest.
Arguments:
- template: float32 [32, 512, 512], P('gz', 'gy'), may hold values from -4 to 4
- target_image: float32 [32, 512, 512], P('gz', 'gy'), may hold values from -4 to 4
- departure_shifts: int32 [4, 3, 32, 512, 512], P(None, None, 'gz', 'gy'), may hold values from -2 to 1
- departure_fractions: float32 [4, 3], replicated, may hold values from 0.1 to 0.9
Outputs:
- update: float32 [3, 32, 512, 512], P(None, 'gz', 'gy')
- deformed: float32 [32, 512, 512], P('gz', 'gy')
The draws below stay inside these ranges and needn't reach their ends.
All inputs are finite; a program needn't handle non-finite values.
Results may differ from the reference program's by a relative error of at most 0.00029.
Values sent between devices are 32-bit elements; how exact they have to be, the bound alone decides.
No kernel may reach another device: no remote copies, remote signals or barrier semaphores. Data moves between devices by JAX's collectives and lax.ppermute only.
A program may use at most 128 MiB of HBM per device.

```python
import jax
import jax.numpy as jnp
from jax import lax

NX = 512
STEPS = 4
CHEB = 8
NY = 512
NZ = 32


def draw_template(key, part):
    rough = jnp.clip(jax.random.normal(key, (NZ, NY, NX), jnp.float32), -4.0, 4.0)
    return rough


def with_ends(values, stream_key, least, high):
    spot = [jax.random.randint(jax.random.fold_in(stream_key, axis), (), 0, length) for axis, length in enumerate(values.shape)]
    longest = values.shape.index(max(values.shape))
    neighbour = spot[:longest] + [(spot[longest] + 1) % values.shape[longest]] + spot[longest + 1:]
    return values.at[tuple(spot)].set(least).at[tuple(neighbour)].set(high)


def levels(rng, shape, shards, smallest, largest):
    factor_of, own = 1.0, jax.random.fold_in(rng, 6)
    for dim, shards_of in shards:
        heights = jnp.exp(jax.random.uniform(jax.random.fold_in(own, dim), (shards_of,), jnp.float32, smallest / len(shards), largest / len(shards)))
        factor_of = factor_of * jnp.repeat(heights, shape[dim] // shards_of).reshape([-1 if axis == dim else 1 for axis in range(len(shape))])
    return factor_of


def centred(key, shape, scale, limit, split=(), held_as=jnp.bfloat16):
    array = jax.random.normal(key, shape, jnp.float32) * scale
    if len(split) > 0:
        array = levels(key, shape, split, -0.22, 0.18) * array
    return jnp.clip(array, min=-limit, max=limit).astype(held_as)


def setup_inputs(seed: int = 0) -> dict:
    key_of = jax.random.split(jax.random.key(seed), 5)
    return {
        "template": draw_template(jax.random.fold_in(key_of[4], 71), 0),
        "target_image": centred(key_of[1], (NZ, NY, NX), 1.0, 4.0, ((0, 8), (1, 32)), jnp.float32),
        "departure_shifts": with_ends(jax.random.randint(key_of[2], (STEPS, 3, NZ, NY, NX), -2, 2), jax.random.fold_in(key_of[2], 1), -2, 1).astype(jnp.int32),
        "departure_fractions": jnp.clip(jax.random.uniform(key_of[3], (STEPS, 3), jnp.float32, 0.1, 0.9), 0.1, 0.9),
    }


DAMPING = 0.25
ACROSS_WEIGHT = 0.0625
ALONG_SCALE = 32.0
SHIFT = 0.25


def cubic_weights(fraction):
    return (-fraction * (fraction - 1.0) * (fraction - 2.0) / 6.0,
            (fraction + 1.0) * (fraction - 1.0) * (fraction - 2.0) / 2.0,
            -(fraction + 1.0) * fraction * (fraction - 2.0) / 2.0,
            (fraction + 1.0) * fraction * (fraction - 1.0) / 6.0)


def advect_axis(field, shifts, fraction, axis):
    weights = cubic_weights(fraction)
    filtered = weights[0] * jnp.roll(field, 1, axis)
    for node in range(1, 4):
        filtered = filtered + weights[node] * jnp.roll(field, 1 - node, axis)
    result = jnp.roll(filtered, -1, axis)
    for offset in (0, -1, -2):
        result = jnp.where(shifts == offset, jnp.roll(filtered, -offset, axis), result)
    return result


def spectral_gain(length_y, freq_x, length_x):
    freq_y = jnp.arange(length_y).astype(jnp.float32)
    sine_y = jnp.sin(jnp.pi * freq_y / length_y) ** 2
    sine_x = jnp.sin(jnp.pi * freq_x.astype(jnp.float32) / length_x) ** 2
    weight_y = (length_y / ALONG_SCALE) ** 2
    return 1.0 / (DAMPING + 4.0 * (weight_y * sine_y[:, None] + ACROSS_WEIGHT * sine_x[None, :]))


def operate_coarse(field):
    beside = jnp.roll(field, -1, 1) + jnp.roll(field, 1, 1)
    beside = beside + jnp.roll(field, -1, 2) + jnp.roll(field, 1, 2)
    beside = beside + jnp.roll(field, -1, 3) + jnp.roll(field, 1, 3)
    return (SHIFT + 6.0) * field - beside


def chebyshev(rhs, operate, count):
    low = SHIFT
    high = SHIFT + 12.0
    theta = (high + low) / 2.0
    delta = (high - low) / 2.0
    sigma = theta / delta
    ratio_now = 1.0 / sigma
    residual = rhs
    direction = rhs / theta
    solution = jnp.zeros_like(rhs)
    for turn in range(count):
        solution = solution + direction
        if turn + 1 < count:
            residual = residual - operate(direction)
            ratio_next = 1.0 / (2.0 * sigma - ratio_now)
            direction = (ratio_next * ratio_now) * direction + (2.0 * ratio_next / delta) * residual
            ratio_now = ratio_next
    return solution


def reference(template, target_image, departure_shifts, departure_fractions):
    image = template
    for step in range(STEPS):
        image = advect_axis(image, departure_shifts[step, 0], departure_fractions[step, 0], 2)
        image = advect_axis(image, departure_shifts[step, 1], departure_fractions[step, 1], 1)
        image = advect_axis(image, departure_shifts[step, 2], departure_fractions[step, 2], 0)
    grad_x = (jnp.roll(image, -1, 2) - jnp.roll(image, 1, 2)) * 0.5
    grad_y = (jnp.roll(image, -1, 1) - jnp.roll(image, 1, 1)) * 0.5
    grad_z = (jnp.roll(image, -1, 0) - jnp.roll(image, 1, 0)) * 0.5
    mismatch = image - target_image
    forces = jnp.stack([mismatch * grad_x, mismatch * grad_y, mismatch * grad_z])
    gain = spectral_gain(NY, jnp.arange(NX), NX)

    def smooth_one(force):
        spectrum = jnp.fft.fft2(force, axes=(1, 2))
        return jnp.real(jnp.fft.ifft2(spectrum * gain, axes=(1, 2))).astype(force.dtype)

    smooth = lax.map(smooth_one, forces)
    coarse = forces.reshape(3, NZ // 2, 2, NY // 2, 2, NX // 2, 2).mean(axis=(2, 4, 6))
    solved = chebyshev(coarse, operate_coarse, CHEB)
    fine = jnp.repeat(jnp.repeat(jnp.repeat(solved, 2, 1), 2, 2), 2, 3)
    update = -(smooth + fine)
    return update, image
```

```python
import jax
import jax.numpy as jnp
import numpy as np
from jax import lax
from jax.sharding import PartitionSpec as P

NX = 512
CHEB = 8
DAMPING = 0.25
ACROSS_WEIGHT = 0.0625
ALONG_SCALE = 32.0
SHIFT = 0.25
HIGH = lax.Precision.HIGH


def hartley(length):
    index = np.arange(length)
    angle = 2.0 * np.pi / length * (np.outer(index, index) % length)
    return (np.cos(angle) + np.sin(angle)) / np.sqrt(length)


def smoother_tables(length_y, length_x, rows):
    weight = (length_y / ALONG_SCALE) ** 2
    sine = np.sin(np.pi * np.arange(length_x) / length_x) ** 2
    a = DAMPING + 4.0 * ACROSS_WEIGHT * sine
    root = np.sqrt(a * a + 4.0 * weight * a)
    r = 2.0 * weight / (a + 2.0 * weight + root)
    y = np.arange(rows)
    local = r ** np.abs(y[:, None, None] - y[None, :, None]) / root
    down = r ** (rows - 1 - y)[:, None]
    up = r ** y[:, None]
    ends = np.stack([down, up])
    spread = np.stack([r ** (y + 1)[:, None], r ** (rows - y)[:, None]]) / root
    return local, ends, spread, r**rows, 1.0 / (1.0 - r**length_y)


def chebyshev_stencil(length_x):
    center = SHIFT + 6.0 - 2.0 * np.cos(2.0 * np.pi * np.arange(length_x) / length_x)
    reach = CHEB - 1
    size = 2 * reach + 1
    rhs = np.zeros((size, size, length_x))
    rhs[reach, reach] = 1.0

    def operate(field):
        wide = np.pad(field, ((1, 1), (1, 1), (0, 0)))
        beside = wide[2:, 1:-1] + wide[:-2, 1:-1] + wide[1:-1, 2:] + wide[1:-1, :-2]
        return center * field - beside

    low = SHIFT
    high = SHIFT + 12.0
    theta = (high + low) / 2.0
    delta = (high - low) / 2.0
    sigma = theta / delta
    ratio_now = 1.0 / sigma
    residual = rhs
    direction = rhs / theta
    result = np.zeros_like(rhs)
    for turn in range(CHEB):
        result = result + direction
        if turn + 1 < CHEB:
            residual = residual - operate(direction)
            ratio_next = 1.0 / (2.0 * sigma - ratio_now)
            direction = ratio_next * ratio_now * direction + 2.0 * ratio_next / delta * residual
            ratio_now = ratio_next
    return result[reach:, reach:]


def ring(axis, offset):
    peers = lax.axis_size(axis)
    return [(i, (i + offset) % peers) for i in range(peers)]


def shift_to(x, axis, offset):
    return lax.ppermute(x, axis, ring(axis, offset))


def rows_of(x, start, stop, dim):
    return lax.slice_in_dim(x, start, stop, axis=dim)


def weights_of(fraction):
    f = fraction
    return jnp.stack(
        [
            -f * (f - 1.0) * (f - 2.0) / 6.0,
            (f + 1.0) * (f - 1.0) * (f - 2.0) / 2.0,
            -(f + 1.0) * f * (f - 2.0) / 2.0,
            (f + 1.0) * f * (f - 1.0) / 6.0,
        ]
    )


def pass_x(field, shifts, w):
    filtered = w[0] * jnp.roll(field, 1, 2)
    for node in range(1, 4):
        filtered = filtered + w[node] * jnp.roll(field, 1 - node, 2)
    result = jnp.roll(filtered, -1, 2)
    for offset in (0, -1, -2):
        result = jnp.where(shifts == offset, jnp.roll(filtered, -offset, 2), result)
    return result


def pass_padded(padded, shifts, w, dim):
    length = padded.shape[dim] - 6
    filtered = w[0] * rows_of(padded, 0, length + 3, dim)
    for node in range(1, 4):
        filtered = filtered + w[node] * rows_of(padded, node, node + length + 3, dim)
    result = rows_of(filtered, 3, 3 + length, dim)
    for offset in (0, -1, -2):
        part = rows_of(filtered, offset + 2, offset + 2 + length, dim)
        result = jnp.where(shifts == offset, part, result)
    return result


def halo_plan(groups, last):
    plan = []
    for number, group in enumerate(groups):
        halo = last if number == len(groups) - 1 else 0
        needs = []
        for step in reversed(group):
            needs.append((step, 2, halo))
            needs.append((step, 1, halo))
            halo = halo + 3
            if step != group[0]:
                needs.append((step, 0, halo))
        plan.append((halo, needs[::-1]))
    return plan


def transport(template, shifts, fractions):
    w = lax.optimization_barrier(weights_of(fractions))
    depth, height = template.shape[0], template.shape[1]
    groups = ((0, 1), (2, 3))
    plan = halo_plan(groups, 1)
    known = {}

    def widened(step, way):
        own = shifts[step, way]
        if (step, way) not in known:
            return own
        before, after = known[step, way]
        return jnp.concatenate([before, own.astype(jnp.float32), after], axis=1)

    image = template
    for number, group in enumerate(groups):
        halo = plan[number][0]
        image = pass_x(image, shifts[group[0], 0], w[:, group[0], 0])
        send = [(None, halo)]
        if number == 0:
            for _, needs in plan:
                send += [((step, way), count) for step, way, count in needs if count > 0]
        lows, highs = [], []
        for what, count in send:
            source = image if what is None else shifts[what].astype(jnp.float32)
            lows.append(rows_of(source, 0, count, 1))
            highs.append(rows_of(source, height - count, height, 1))
        low = lows[0] if len(lows) == 1 else jnp.concatenate(lows, axis=1)
        high = highs[0] if len(highs) == 1 else jnp.concatenate(highs, axis=1)
        before = shift_to(high, "gy", 1)
        after = shift_to(low, "gy", -1)
        place = 0
        for what, count in send:
            pair = (rows_of(before, place, place + count, 1), rows_of(after, place, place + count, 1))
            place = place + count
            if what is None:
                image = jnp.concatenate([pair[0], image, pair[1]], axis=1)
            else:
                known[what] = pair
        if number == 0:
            last = shifts[groups[-1][-1], 2]
            shift_before = shift_to(last[depth - 1 :], "gz", 1)
            shift_after = shift_to(last[:1], "gz", -1)
        for step in group:
            if step != group[0]:
                image = pass_x(image, widened(step, 0), w[:, step, 0])
            image = pass_padded(image, widened(step, 1), w[:, step, 1], 1)
            layers = 3
            moves = widened(step, 2)
            if step == groups[-1][-1]:
                layers = 4
                sides = ((0, 0), (1, 1), (0, 0))
                moves = jnp.concatenate(
                    [
                        jnp.pad(shift_before.astype(jnp.float32), sides),
                        moves,
                        jnp.pad(shift_after.astype(jnp.float32), sides),
                    ],
                    axis=0,
                )
            before = shift_to(image[depth - layers :], "gz", 1)
            after = shift_to(image[:layers], "gz", -1)
            padded = jnp.concatenate([before, image, after], axis=0)
            image = pass_padded(padded, moves, w[:, step, 2], 0)
    return image


def dot(a, b):
    return jnp.dot(a, b, precision=HIGH, preferred_element_type=jnp.float32)


def on_device(template, target_image, departure_shifts, departure_fractions):
    depth, height = template.shape[0], template.shape[1]
    peers_y = lax.axis_size("gy")
    length_y = height * peers_y
    framed = transport(template, departure_shifts, departure_fractions)
    image = framed[1:-1, 1:-1]
    grad_x = (jnp.roll(image, -1, 2) - jnp.roll(image, 1, 2)) * 0.5
    grad_y = (framed[1:-1, 2:, :] - framed[1:-1, :-2, :]) * 0.5
    grad_z = (framed[2:, 1:-1, :] - framed[:-2, 1:-1, :]) * 0.5
    mismatch = image - target_image
    forces = jnp.stack([mismatch * grad_x, mismatch * grad_y, mismatch * grad_z])
    rows = 3 * depth * height
    flat = forces.reshape(rows, NX)

    f32 = lambda table: jnp.asarray(table, jnp.float32)
    fine_x = hartley(NX)
    coarse_x = np.repeat(hartley(NX // 2), 2, axis=0)
    spectrum = dot(flat, f32(fine_x))
    local, ends, spread, ratio, wrap = smoother_tables(length_y, NX, height)
    lines = spectrum.reshape(3 * depth, height, NX)

    pair_z = np.kron(np.eye(depth // 2), np.ones((1, 2)))
    pair_y = np.kron(np.eye(height // 2), np.ones((1, 2)))
    pairs = np.kron(np.eye(3), np.kron(pair_z, pair_y))
    coarse = dot(f32(pairs / 8.0), dot(flat, f32(coarse_x)))
    coarse = coarse.reshape(3, depth // 2, height // 2, NX // 2)

    reach = CHEB - 1
    coarse_before = shift_to(coarse[:, :, height // 2 - reach :], "gy", 1)
    coarse_after = shift_to(coarse[:, :, :reach], "gy", -1)

    tails = jnp.stack(
        [jnp.sum(lines * f32(ends[0]), axis=1), jnp.sum(lines * f32(ends[1]), axis=1)]
    )
    lanes = 128
    across = NX // lanes
    groups = peers_y // across
    share = 2 * 3 * depth // groups
    parcels = tails.reshape(groups, share, across, lanes).transpose(0, 2, 1, 3)
    parcels = parcels.reshape(peers_y, share, lanes)
    carried = lax.all_to_all(parcels, "gy", 0, 0, tiled=True)
    place = lax.axis_index("gy")
    forward = place // across < groups // 2
    tables = f32(np.stack([ratio, wrap]).reshape(2, across, 1, lanes))
    tables = lax.dynamic_index_in_dim(tables, place % across, axis=1, keepdims=False)
    power, scale = tables[0], tables[1]
    sums = carried
    sums = jnp.where(forward, jnp.roll(sums, 1, 0), jnp.roll(sums, -1, 0)) * scale
    reach_y = 1
    while reach_y < peers_y:
        beside = jnp.where(forward, jnp.roll(sums, reach_y, 0), jnp.roll(sums, -reach_y, 0))
        sums = sums + power * beside
        power = power * power
        reach_y = reach_y * 2
    returned = lax.all_to_all(sums, "gy", 0, 0, tiled=True)
    carries = returned.reshape(groups, across, share, lanes).transpose(0, 2, 1, 3)
    carries = carries.reshape(2, 3 * depth, NX)

    smooth = f32(local[0]) * lines[:, 0:1]
    for y in range(1, height):
        smooth = smooth + f32(local[y]) * lines[:, y : y + 1]

    wide = jnp.concatenate([coarse_before, coarse, coarse_after], axis=2)
    stencil = f32(chebyshev_stencil(NX // 2))
    half = height // 2
    sides = [wide[:, :, reach : reach + half]]
    for k in range(1, reach + 1):
        sides.append(wide[:, :, reach - k : reach - k + half] + wide[:, :, reach + k : reach + k + half])
    layers = []
    for dz in range(reach + 1):
        total = stencil[dz, 0] * sides[0]
        for k in range(1, reach + 1 - dz):
            total = total + stencil[dz, k] * sides[k]
        layers.append(total)

    def term(z):
        total = None
        for layer in range(depth // 2):
            away = abs(z - layer)
            if away <= reach:
                part = layers[away][:, layer]
                total = part if total is None else total + part
        return total

    peers_z = lax.axis_size("gz")
    count_z = peers_z * depth // 2
    own = depth // 2

    def block(offset):
        parts = []
        for layer in range(own):
            z = offset * own + layer
            terms = [term(v) for v in (z - count_z, z, z + count_z)]
            terms = [t for t in terms if t is not None]
            total = terms[0]
            for t in terms[1:]:
                total = total + t
            parts.append(total)
        return jnp.stack(parts, axis=1)

    solved = block(0)
    for offset in range(1, peers_z):
        near = offset if offset <= peers_z // 2 else offset - peers_z
        solved = solved + shift_to(block(near), "gz", near)

    solved = solved.reshape(rows // 4, NX // 2)
    solved = dot(f32(pairs.T), solved)
    smooth = smooth + f32(spread[0]) * carries[0][:, None] + f32(spread[1]) * carries[1][:, None]
    smooth = smooth.reshape(rows, NX)
    update = dot(smooth, f32(-fine_x)) + dot(solved, f32(-coarse_x.T))
    return (update.reshape(3, depth, height, NX), image)


def solution(mesh):
    return jax.shard_map(
        on_device,
        mesh=mesh,
        in_specs=(P("gz", "gy", None), P("gz", "gy", None), P(None, None, "gz", "gy", None), P()),
        out_specs=(P(None, "gz", "gy", None), P("gz", "gy", None)),
        check_vma=False,
    )
```

```python
import functools

import jax
import jax.numpy as jnp
import ml_dtypes
import numpy as np
from jax import lax
from jax.experimental import pallas as pl
from jax.experimental.pallas import tpu as pltpu
from jax.sharding import PartitionSpec as P

NX = 512
CHEB = 8
DAMPING = 0.25
ACROSS_WEIGHT = 0.0625
ALONG_SCALE = 32.0
SHIFT = 0.25
HIGH = lax.Precision.HIGH


def hartley(length):
    index = np.arange(length)
    angle = 2.0 * np.pi / length * (np.outer(index, index) % length)
    return (np.cos(angle) + np.sin(angle)) / np.sqrt(length)


def smoother_tables(length_y, length_x, rows):
    weight = (length_y / ALONG_SCALE) ** 2
    sine = np.sin(np.pi * np.arange(length_x) / length_x) ** 2
    a = DAMPING + 4.0 * ACROSS_WEIGHT * sine
    root = np.sqrt(a * a + 4.0 * weight * a)
    r = 2.0 * weight / (a + 2.0 * weight + root)
    y = np.arange(rows)
    local = r ** np.abs(y[:, None, None] - y[None, :, None]) / root
    down = r ** (rows - 1 - y)[:, None]
    up = r ** y[:, None]
    ends = np.stack([down, up])
    spread = np.stack([r ** (y + 1)[:, None], r ** (rows - y)[:, None]]) / root
    return local, ends, spread, r**rows, 1.0 / (1.0 - r**length_y)


def chebyshev_stencil(length_x):
    center = SHIFT + 6.0 - 2.0 * np.cos(2.0 * np.pi * np.arange(length_x) / length_x)
    reach = CHEB - 1
    size = 2 * reach + 1
    rhs = np.zeros((size, size, length_x))
    rhs[reach, reach] = 1.0

    def operate(field):
        wide = np.pad(field, ((1, 1), (1, 1), (0, 0)))
        beside = wide[2:, 1:-1] + wide[:-2, 1:-1] + wide[1:-1, 2:] + wide[1:-1, :-2]
        return center * field - beside

    low = SHIFT
    high = SHIFT + 12.0
    theta = (high + low) / 2.0
    delta = (high - low) / 2.0
    sigma = theta / delta
    ratio_now = 1.0 / sigma
    residual = rhs
    direction = rhs / theta
    result = np.zeros_like(rhs)
    for turn in range(CHEB):
        result = result + direction
        if turn + 1 < CHEB:
            residual = residual - operate(direction)
            ratio_next = 1.0 / (2.0 * sigma - ratio_now)
            direction = ratio_next * ratio_now * direction + 2.0 * ratio_next / delta * residual
            ratio_now = ratio_next
    return result[reach:, reach:]


def ring(axis, offset):
    peers = lax.axis_size(axis)
    return [(i, (i + offset) % peers) for i in range(peers)]


def shift_to(x, axis, offset):
    return lax.ppermute(x, axis, ring(axis, offset))


def cubic_weights(f):
    return (
        -f * (f - 1.0) * (f - 2.0) * (1.0 / 6.0),
        (f + 1.0) * (f - 1.0) * (f - 2.0) * 0.5,
        -(f + 1.0) * f * (f - 2.0) * 0.5,
        (f + 1.0) * f * (f - 1.0) * (1.0 / 6.0),
    )


def blend(w, parts):
    total = w[0] * parts[0]
    for node in range(1, 4):
        total = total + w[node] * parts[node]
    return total


def choose(moves, parts):
    result = parts[3]
    for offset in (0, -1, -2):
        result = jnp.where(moves == offset, parts[offset + 2], result)
    return result


def x_pass(field, moves, w):
    turn = lambda value, by: value if by == 0 else pltpu.roll(value, by % NX, 1)
    filtered = blend(w, [turn(field, 1 - node) for node in range(4)])
    return choose(moves, [turn(filtered, -offset) for offset in (-2, -1, 0, 1)])


def y_pass(padded_ref, filtered_ref, layer, rows, moves, w):
    parts = [padded_ref[layer, node : node + rows + 3, :] for node in range(4)]
    filtered_ref[layer, 0 : rows + 3, :] = blend(w, parts)
    return choose(moves, [filtered_ref[layer, k : k + rows, :] for k in range(4)])


def z_filter(layers, filtered_ref, w):
    for m in range(len(layers) - 3):
        filtered_ref[m] = blend(w, [layers[m + node]() for node in range(4)])


def layers_of(before_ref, field_ref, after_ref, count):
    return [
        functools.partial(lambda ref, i: ref[i], ref, i)
        for ref, layers in ((before_ref, count), (field_ref, field_ref.shape[0]), (after_ref, count))
        for i in range(layers)
    ]


def weights_at(fractions_ref, step, way):
    return cubic_weights(fractions_ref[step, way])


def padded_rows(count):
    return -(-count // 8) * 8


def store_wide(wide_ref, layer, before, own, after):
    place = 0
    for part in (before, own, after):
        if part is not None:
            wide_ref[layer, place : place + part.shape[0], :] = part
            place = place + part.shape[0]
    rest = wide_ref.shape[1] - place
    if rest > 0:
        wide_ref[layer, place:, :] = jnp.zeros((rest, NX), wide_ref.dtype)


class Plan:
    def __init__(self, last):
        self.halos = {}
        halo = last
        for step in (3, 2):
            self.halos[step, 2] = self.halos[step, 1] = halo
            halo = halo + 3
            if step == 3:
                self.halos[step, 0] = halo
        self.second = halo
        halo = 0
        for step in (1, 0):
            self.halos[step, 2] = self.halos[step, 1] = halo
            halo = halo + 3
            if step == 1:
                self.halos[step, 0] = halo
        self.first = halo
        self.places = {}
        place = self.first
        for key in sorted(self.halos):
            if self.halos[key] > 0:
                self.places[key] = place
                place = place + self.halos[key]
        self.total = place

    def moves(self, refs, key, layer, wide_ref):
        before_ref, after_ref, shifts_ref = refs
        own = shifts_ref[key[0], key[1], layer]
        if key not in self.places:
            return own
        start, stop = self.places[key], self.places[key] + self.halos[key]
        store_wide(
            wide_ref,
            layer,
            before_ref[layer, start:stop, :],
            own.astype(jnp.float32),
            after_ref[layer, start:stop, :],
        )
        return wide_ref[layer]


PLAN = Plan(1)
HEIGHT = 16


def copies_of(pairs, sems):
    copies = [pltpu.make_async_copy(source, place, sems.at[i]) for i, (source, place) in enumerate(pairs)]
    for copy in copies:
        copy.start()
    return copies


def start_kernel(image_hbm, shifts_hbm, fractions_hbm, out_ref, low_ref, high_ref,
                 image_ref, shifts_ref, fractions_ref, sems):
    copies = copies_of(
        ((fractions_hbm, fractions_ref), (image_hbm, image_ref), (shifts_hbm, shifts_ref)), sems
    )
    for copy in copies:
        copy.wait()
    w = weights_at(fractions_ref, 0, 0)
    depth = image_ref.shape[0]
    for layer in range(depth):
        out_ref[layer] = x_pass(image_ref[layer], shifts_ref[0, 0, layer], w)
        low_ref[layer, 0 : PLAN.first, :] = out_ref[layer, 0 : PLAN.first, :]
        high_ref[layer, 0 : PLAN.first, :] = out_ref[layer, HEIGHT - PLAN.first :, :]
        for key, place in PLAN.places.items():
            count = PLAN.halos[key]
            source = shifts_ref.at[key[0], key[1], layer]
            low_ref[layer, place : place + count, :] = source[0:count, :].astype(jnp.float32)
            high_ref[layer, place : place + count, :] = source[HEIGHT - count :, :].astype(jnp.float32)


def y_kernel(step, image_ref, low_ref, high_ref, before_ref, after_ref, shifts_ref, fractions_ref,
             out_ref, padded_ref, filtered_ref, wide_ref):
    rows = out_ref.shape[1]
    w = weights_at(fractions_ref, step, 1)
    depth = image_ref.shape[0]
    halo = PLAN.halos[step, 1] + 3
    for layer in range(depth):
        store_wide(
            padded_ref, layer, low_ref[layer, 0:halo, :], image_ref[layer], high_ref[layer, 0:halo, :]
        )
        moves = PLAN.moves((before_ref, after_ref, shifts_ref), (step, 1), layer, wide_ref)
        out_ref[layer] = y_pass(padded_ref, filtered_ref, layer, rows, moves, w)


def z_x_y_kernel(step, rows_out, below_ref, image_ref, above_ref, before_ref, after_ref, shifts_ref,
                 fractions_ref, *rest):
    *outs, padded_ref, filtered_y_ref, filtered_ref, wide_ref = rest
    refs = (before_ref, after_ref, shifts_ref)
    depth = image_ref.shape[0]
    z_filter(layers_of(below_ref, image_ref, above_ref, 3), filtered_ref, weights_at(fractions_ref, step, 2))
    wx = weights_at(fractions_ref, step + 1, 0)
    wy = weights_at(fractions_ref, step + 1, 1)
    rows = image_ref.shape[1]
    for layer in range(depth):
        moves = PLAN.moves(refs, (step, 2), layer, wide_ref)
        value = choose(moves, [filtered_ref[layer + k] for k in range(4)])
        moves = PLAN.moves(refs, (step + 1, 0), layer, wide_ref)
        value = x_pass(value, moves, wx)
        if rows_out is None:
            outs[0][layer] = value
            outs[1][layer, 0 : PLAN.second, :] = outs[0][layer, 0 : PLAN.second, :]
            outs[2][layer, 0 : PLAN.second, :] = outs[0][layer, HEIGHT - PLAN.second :, :]
            continue
        padded_ref[layer, 0:rows, :] = value
        padded_ref[layer, rows:, :] = jnp.zeros((padded_ref.shape[1] - rows, NX), jnp.float32)
        moves = PLAN.moves(refs, (step + 1, 1), layer, wide_ref.at[:, 0:rows_out, :])
        value = y_pass(padded_ref, filtered_y_ref, layer, rows_out, moves, wy)
        outs[0][layer] = value
        if len(outs) > 1:
            if layer < 3:
                outs[1][layer] = value
            if layer >= depth - 3:
                outs[2][layer - depth + 3] = value
    if len(outs) > 1 and rows_out is not None:
        outs[1][3] = shifts_ref[3, 2, 0].astype(jnp.float32)
        outs[2][3] = shifts_ref[3, 2, depth - 1].astype(jnp.float32)


def split(x):
    high = x.astype(jnp.bfloat16)
    return high, (x - high.astype(jnp.float32)).astype(jnp.bfloat16)


def product(a, b):
    return jnp.dot(a, b, preferred_element_type=jnp.float32)


def force_kernel(below_ref, image_ref, above_ref, before_ref, after_ref, shifts_ref, fractions_ref,
                 first_ref, last_ref, target_hbm, table_high_hbm, table_low_hbm, pairs_hbm, ends_hbm,
                 out_ref, spectrum_ref, coarse_ref, parcels_ref, filtered_ref, wide_ref, frame_ref, force_ref,
                 target_ref, table_high_ref, table_low_ref, pairs_ref, ends_ref, sems):
    copies = copies_of(
        (
            (target_hbm, target_ref),
            (table_high_hbm, table_high_ref),
            (table_low_hbm, table_low_ref),
            (pairs_hbm, pairs_ref),
            (ends_hbm, ends_ref),
        ),
        sems,
    )
    refs = (before_ref, after_ref, shifts_ref)
    depth = image_ref.shape[0]
    z_filter(layers_of(below_ref, image_ref, above_ref, 4), filtered_ref, weights_at(fractions_ref, 3, 2))
    own = slice(1, 1 + HEIGHT)
    outer = []
    for moves_ref, base in ((first_ref, 0), (last_ref, depth + 1)):
        outer.append(choose(moves_ref[3], [filtered_ref[base + k, own, :] for k in range(4)]))
    for layer in range(depth):
        moves = PLAN.moves(refs, (3, 2), layer, wide_ref)
        frame_ref[layer] = choose(moves, [filtered_ref[layer + 1 + k] for k in range(4)])
    copies[0].wait()
    for layer in range(depth):
        image = frame_ref[layer, own, :]
        out_ref[layer] = image
        miss = (image - target_ref[layer]) * 0.5
        below = outer[0] if layer == 0 else frame_ref[layer - 1, own, :]
        above = outer[1] if layer == depth - 1 else frame_ref[layer + 1, own, :]
        slopes = (
            pltpu.roll(image, NX - 1, 1) - pltpu.roll(image, 1, 1),
            frame_ref[layer, 2 : 2 + HEIGHT, :] - frame_ref[layer, 0:HEIGHT, :],
            above - below,
        )
        for way in range(3):
            place = (way * depth + layer) * HEIGHT
            force_ref[place : place + HEIGHT, :] = miss * slopes[way]
    for copy in copies[1:]:
        copy.wait()
    high, low = split(force_ref[...])
    result = product(high, table_high_ref[...])
    result = result + product(high, table_low_ref[...])
    result = result + product(low, table_high_ref[...])
    spectrum_ref[...] = result[:, :NX]
    high, low = split(result[:, NX:])
    coarse = product(pairs_ref[...], high) + product(pairs_ref[...], low)
    coarse_ref[...] = coarse.reshape(coarse_ref.shape)
    share = parcels_ref.shape[1]
    across = NX // 128
    for side in range(2):
        for line in range(3 * depth):
            part = spectrum_ref[line * HEIGHT : (line + 1) * HEIGHT, :] * ends_ref[side]
            row = jnp.sum(part, axis=0, keepdims=True)
            place = side * 3 * depth + line
            for lane in range(across):
                parcel = place // share * across + lane
                parcels_ref[parcel, place % share, :] = row[0, lane * 128 : (lane + 1) * 128]


def carry_kernel(place_ref, carried_ref, tables_ref, out_ref):
    peers = carried_ref.shape[0]
    across = NX // 128
    place = place_ref[0]
    forward = place < peers // 2
    table = tables_ref[lax.rem(place, across)]
    power, scale = table[0:1], table[1:2]

    def sums_of(turn, power):
        sums = turn(carried_ref[...], 1) * scale[None]
        reach = 1
        while reach < peers:
            sums = sums + power[None] * turn(sums, reach)
            power = power * power
            reach = reach * 2
        return sums

    @pl.when(forward)
    def _():
        out_ref[...] = sums_of(lambda x, k: jnp.concatenate([x[peers - k :], x[: peers - k]]), power)

    @pl.when(jnp.logical_not(forward))
    def _():
        out_ref[...] = sums_of(lambda x, k: jnp.concatenate([x[k:], x[:k]]), power)


def stencil_kernel(low_ref, before_ref, own_ref, after_ref, high_ref, stencil_ref,
                   out_ref, up_ref, down_ref, wide_ref):
    reach = CHEB - 1
    ways = own_ref.shape[0]
    layers = own_ref.shape[1]
    half = own_ref.shape[2]
    for way in range(ways):
        column = [
            functools.partial(lambda ref, i: ref[way, i], ref, i)
            for ref in (low_ref, before_ref, own_ref, after_ref, high_ref)
            for i in range(ref.shape[1])
        ]
        for layer in range(layers):
            center = reach + layer
            sums = [column[center]()]
            for k in range(1, reach + 1):
                sums.append(column[center - k]() + column[center + k]())
            wide_ref[way, layer] = jnp.zeros((3 * half, NX // 2), jnp.float32)
            for dy in range(reach + 1):
                total = stencil_ref[0, dy : dy + 1, :] * sums[0]
                for dz in range(1, reach + 1 - dy):
                    total = total + stencil_ref[dz, dy : dy + 1, :] * sums[dz]
                for sign in (-1, 1) if dy > 0 else (1,):
                    rows = slice(half + sign * dy, 2 * half + sign * dy)
                    wide_ref[way, layer, rows, :] += total
            up_ref[way, layer] = wide_ref[way, layer, 0:half, :]
            out_ref[way, layer] = wide_ref[way, layer, half : 2 * half, :]
            down_ref[way, layer] = wide_ref[way, layer, 2 * half :, :]


def call(kernel, outs, scratch, *args, smem=(), hbm=(), copies=0):
    vmem = pl.BlockSpec(memory_space=pltpu.VMEM)
    spaces = {i: pltpu.SMEM for i in smem} | {i: pltpu.HBM for i in hbm}
    specs = [pl.BlockSpec(memory_space=spaces.get(i, pltpu.VMEM)) for i in range(len(args))]
    shape = lambda dims: jax.ShapeDtypeStruct(dims, jnp.float32)
    scratch = [pltpu.VMEM(dims, jnp.float32) if isinstance(dims, tuple) else dims for dims in scratch]
    if copies:
        scratch.append(pltpu.SemaphoreType.DMA((copies,)))
    return pl.pallas_call(
        kernel,
        out_shape=tuple(shape(dims) for dims in outs),
        in_specs=specs,
        out_specs=tuple(vmem for _ in outs),
        scratch_shapes=scratch,
        compiler_params=pltpu.CompilerParams(vmem_limit_bytes=12 * 2**20),
    )(*args)


def f32(table):
    return jnp.asarray(table, jnp.float32)


def bf16_pair(table):
    high = np.asarray(table, np.float32).astype(ml_dtypes.bfloat16)
    low = (np.asarray(table, np.float64) - high.astype(np.float64)).astype(ml_dtypes.bfloat16)
    return jnp.asarray(high), jnp.asarray(low)


def dot(a, b):
    return jnp.dot(a, b, precision=HIGH, preferred_element_type=jnp.float32)


def on_device(template, target_image, departure_shifts, departure_fractions):
    depth, height = template.shape[0], template.shape[1]
    peers_y = lax.axis_size("gy")
    length_y = height * peers_y
    shifts, fractions = departure_shifts, departure_fractions
    block = lambda layers, rows: (layers, padded_rows(rows), NX)
    full = (depth, height, NX)

    image, low, high = call(
        start_kernel,
        [full, (depth, PLAN.total, NX), (depth, PLAN.total, NX)],
        [full, pltpu.VMEM(shifts.shape, jnp.int32), pltpu.SMEM(fractions.shape, jnp.float32)],
        template, shifts, fractions, hbm=(0, 1, 2), copies=3,
    )
    before = shift_to(high, "gy", 1)
    after = shift_to(low, "gy", -1)
    halos = (before, after, shifts, fractions)

    def y_step(step, image, low, high):
        rows = padded_rows(height + 2 * PLAN.halos[step, 1])
        (image,) = call(
            functools.partial(y_kernel, step),
            [(depth, rows, NX)],
            [(depth, rows + 8, NX), (depth, rows + 8, NX), (depth, rows, NX)],
            image, low, high, *halos, smem=(6,),
        )
        return image, image[:3], image[depth - 3 :]

    def exchange_z(down, up):
        return shift_to(up, "gz", 1), shift_to(down, "gz", -1)

    def z_step(step, outs, rows_out, below, image, above):
        rows = image.shape[1]
        layers = 3
        return call(
            functools.partial(z_x_y_kernel, step, rows_out),
            outs,
            [(depth, rows + 8, NX), (depth, rows + 8, NX), (depth + 2 * layers - 3, rows, NX), (depth, rows, NX)],
            below, image, above, *halos, smem=(6,),
        )

    image, down, up = y_step(0, image, before, after)
    below, above = exchange_z(down, up)
    image, down, up = z_step(0, [full, full, full], height, below, image, above)
    below, above = exchange_z(down, up)
    outer_low, outer_high = below, above
    edge = (depth, PLAN.second, NX)
    image, low, high = z_step(1, [full, edge, edge], None, below, image, above)
    low, high = shift_to(high, "gy", 1), shift_to(low, "gy", -1)
    image, down, up = y_step(2, image, low, high)
    below, above = exchange_z(down, up)
    rows = padded_rows(height + 2)
    (image,) = z_step(2, [(depth, rows, NX)], rows, below, image, above)
    below, above = exchange_z(image, image)

    half, lanes = NX // 2, 128
    across = NX // lanes
    groups = peers_y // across
    share = 2 * 3 * depth // groups
    fine_x = hartley(NX)
    coarse_x = np.repeat(hartley(half), 2, axis=0)
    local, ends, spread, ratio, wrap = smoother_tables(length_y, NX, height)
    pair_z = np.kron(np.eye(depth // 2), np.ones((1, 2)))
    pair_y = np.kron(np.eye(height // 2), np.ones((1, 2)))
    pairs = np.kron(np.eye(3), np.kron(pair_z, pair_y))
    lines = 3 * depth
    coarse_shape = (3, depth // 2, height // 2, half)
    image, spectrum, coarse, parcels = call(
        force_kernel,
        [full, (lines * height, NX), coarse_shape, (peers_y, share, lanes)],
        [
            (3 * depth - 3, rows, NX), (depth, rows, NX), (depth, rows, NX), (lines * height, NX), full,
            pltpu.VMEM((NX, NX + half), jnp.bfloat16), pltpu.VMEM((NX, NX + half), jnp.bfloat16),
            pltpu.VMEM(pairs.shape, jnp.bfloat16), ends.shape,
        ],
        below, image, above, *halos, outer_low, outer_high, target_image,
        *bf16_pair(np.concatenate([fine_x, coarse_x], axis=1)),
        jnp.asarray(pairs / 8.0, jnp.bfloat16), f32(ends), smem=(6,), hbm=(9, 10, 11, 12, 13), copies=5,
    )

    carried = lax.all_to_all(parcels, "gy", 0, 0, tiled=True)
    coarse_low = shift_to(coarse, "gz", 1)
    coarse_high = shift_to(coarse, "gz", -1)
    far_low = shift_to(jnp.concatenate([coarse_low[:, 1:], coarse, coarse_high], axis=1), "gz", 3)
    far_high = shift_to(jnp.concatenate([coarse_low, coarse, coarse_high[:, :1]], axis=1), "gz", -3)

    carried, far_low, far_high = lax.optimization_barrier((carried, far_low, far_high))
    place = lax.axis_index("gy").reshape(1).astype(jnp.int32)
    tables = f32(np.stack([ratio, wrap]).reshape(2, across, lanes).transpose(1, 0, 2))
    (sums,) = call(carry_kernel, [(peers_y, share, lanes)], [], place, carried, tables, smem=(0,))
    returned = lax.all_to_all(sums, "gy", 0, 0, tiled=True)

    own, up, down = call(
        stencil_kernel,
        [coarse_shape] * 3,
        [(3, depth // 2, 3 * height // 2, half)],
        far_low, coarse_low, coarse, coarse_high, far_high, f32(chebyshev_stencil(half)),
    )
    solved = own + shift_to(up, "gy", -1) + shift_to(down, "gy", 1)

    spectrum = spectrum.reshape(lines, height, NX)
    smooth = f32(local[0]) * spectrum[:, 0:1]
    for y in range(1, height):
        smooth = smooth + f32(local[y]) * spectrum[:, y : y + 1]
    carries = returned.reshape(groups, across, share, lanes).transpose(0, 2, 1, 3)
    carries = carries.reshape(2, lines, NX)
    smooth = smooth + f32(spread[0]) * carries[0][:, None] + f32(spread[1]) * carries[1][:, None]
    smooth = smooth.reshape(lines * height, NX)
    solved = dot(f32(pairs.T), solved.reshape(lines * height // 4, half))
    update = dot(smooth, f32(-fine_x)) + dot(solved, f32(-coarse_x.T))
    return (update.reshape(3, depth, height, NX), image)


def solution(mesh):
    return jax.shard_map(
        on_device,
        mesh=mesh,
        in_specs=(P("gz", "gy", None), P("gz", "gy", None), P(None, None, "gz", "gy", None), P()),
        out_specs=(P(None, "gz", "gy", None), P("gz", "gy", None)),
        check_vma=False,
    )
```

```python
import functools

import jax
import jax.numpy as jnp
import ml_dtypes
import numpy as np
from jax import lax
from jax.experimental import pallas as pl
from jax.experimental.pallas import tpu as pltpu
from jax.sharding import PartitionSpec as P

NX = 512
CHEB = 8
DAMPING = 0.25
ACROSS_WEIGHT = 0.0625
ALONG_SCALE = 32.0
SHIFT = 0.25
HIGH = lax.Precision.HIGH


def hartley(length):
    index = np.arange(length)
    angle = 2.0 * np.pi / length * (np.outer(index, index) % length)
    return (np.cos(angle) + np.sin(angle)) / np.sqrt(length)


def smoother_tables(length_y, length_x, rows):
    weight = (length_y / ALONG_SCALE) ** 2
    sine = np.sin(np.pi * np.arange(length_x) / length_x) ** 2
    a = DAMPING + 4.0 * ACROSS_WEIGHT * sine
    root = np.sqrt(a * a + 4.0 * weight * a)
    r = 2.0 * weight / (a + 2.0 * weight + root)
    y = np.arange(rows)
    local = r ** np.abs(y[:, None, None] - y[None, :, None]) / root
    down = r ** (rows - 1 - y)[:, None]
    up = r ** y[:, None]
    ends = np.stack([down, up])
    spread = np.stack([r ** (y + 1)[:, None], r ** (rows - y)[:, None]]) / root
    return local, ends, spread, r**rows, 1.0 / (1.0 - r**length_y)


def chebyshev_stencil(length_x):
    center = SHIFT + 6.0 - 2.0 * np.cos(2.0 * np.pi * np.arange(length_x) / length_x)
    reach = CHEB - 1
    size = 2 * reach + 1
    rhs = np.zeros((size, size, length_x))
    rhs[reach, reach] = 1.0

    def operate(field):
        wide = np.pad(field, ((1, 1), (1, 1), (0, 0)))
        beside = wide[2:, 1:-1] + wide[:-2, 1:-1] + wide[1:-1, 2:] + wide[1:-1, :-2]
        return center * field - beside

    low = SHIFT
    high = SHIFT + 12.0
    theta = (high + low) / 2.0
    delta = (high - low) / 2.0
    sigma = theta / delta
    ratio_now = 1.0 / sigma
    residual = rhs
    direction = rhs / theta
    result = np.zeros_like(rhs)
    for turn in range(CHEB):
        result = result + direction
        if turn + 1 < CHEB:
            residual = residual - operate(direction)
            ratio_next = 1.0 / (2.0 * sigma - ratio_now)
            direction = ratio_next * ratio_now * direction + 2.0 * ratio_next / delta * residual
            ratio_now = ratio_next
    return result[reach:, reach:]


def ring(axis, offset):
    peers = lax.axis_size(axis)
    return [(i, (i + offset) % peers) for i in range(peers)]


def shift_to(x, axis, offset):
    return lax.ppermute(x, axis, ring(axis, offset))


def cubic_weights(f):
    return (
        -f * (f - 1.0) * (f - 2.0) * (1.0 / 6.0),
        (f + 1.0) * (f - 1.0) * (f - 2.0) * 0.5,
        -(f + 1.0) * f * (f - 2.0) * 0.5,
        (f + 1.0) * f * (f - 1.0) * (1.0 / 6.0),
    )


def blend(w, parts):
    total = w[0] * parts[0]
    for node in range(1, 4):
        total = total + w[node] * parts[node]
    return total


def choose(moves, parts):
    result = parts[3]
    for offset in (0, -1, -2):
        result = jnp.where(moves == offset, parts[offset + 2], result)
    return result


def x_pass(field, moves, w):
    turn = lambda value, by: value if by == 0 else pltpu.roll(value, by % NX, 1)
    filtered = blend(w, [turn(field, 1 - node) for node in range(4)])
    return choose(moves, [turn(filtered, -offset) for offset in (-2, -1, 0, 1)])


def y_pass(padded_ref, filtered_ref, layer, rows, moves, w):
    parts = [padded_ref[layer, node : node + rows + 3, :] for node in range(4)]
    filtered_ref[layer, 0 : rows + 3, :] = blend(w, parts)
    return choose(moves, [filtered_ref[layer, k : k + rows, :] for k in range(4)])


def z_filter(layers, filtered_ref, w):
    for m in range(len(layers) - 3):
        filtered_ref[m] = blend(w, [layers[m + node]() for node in range(4)])


def layers_of(before_ref, field_ref, after_ref, count):
    return [
        functools.partial(lambda ref, i: ref[i], ref, i)
        for ref, layers in ((before_ref, count), (field_ref, field_ref.shape[0]), (after_ref, count))
        for i in range(layers)
    ]


def weights_at(fractions_ref, step, way):
    return cubic_weights(fractions_ref[step, way])


def padded_rows(count):
    return -(-count // 8) * 8


def store_wide(wide_ref, layer, before, own, after):
    place = 0
    for part in (before, own, after):
        if part is not None:
            wide_ref[layer, place : place + part.shape[0], :] = part
            place = place + part.shape[0]
    rest = wide_ref.shape[1] - place
    if rest > 0:
        wide_ref[layer, place:, :] = jnp.zeros((rest, NX), wide_ref.dtype)


class Plan:
    def __init__(self, last):
        self.halos = {}
        halo = last
        for step in (3, 2):
            self.halos[step, 2] = self.halos[step, 1] = halo
            halo = halo + 3
            if step == 3:
                self.halos[step, 0] = halo
        self.second = halo
        halo = 0
        for step in (1, 0):
            self.halos[step, 2] = self.halos[step, 1] = halo
            halo = halo + 3
            if step == 1:
                self.halos[step, 0] = halo
        self.first = halo
        self.places = {}
        place = self.first
        for key in sorted(self.halos):
            if self.halos[key] > 0:
                self.places[key] = place
                place = place + self.halos[key]
        self.total = place

    def moves(self, refs, key, layer, wide_ref):
        before_ref, after_ref, shifts_ref = refs
        own = shifts_ref[key[0], key[1], layer]
        if key not in self.places:
            return own
        start, stop = self.places[key], self.places[key] + self.halos[key]
        store_wide(
            wide_ref,
            layer,
            before_ref[layer, start:stop, :],
            own.astype(jnp.float32),
            after_ref[layer, start:stop, :],
        )
        return wide_ref[layer]


PLAN = Plan(1)
HEIGHT = 16


def copies_of(pairs, sems):
    copies = [pltpu.make_async_copy(source, place, sems.at[i]) for i, (source, place) in enumerate(pairs)]
    for copy in copies:
        copy.start()
    return copies


def start_kernel(image_hbm, shifts_hbm, fractions_hbm, out_ref, low_ref, high_ref,
                 image_ref, shifts_ref, fractions_ref, sems):
    copies = copies_of(
        ((fractions_hbm, fractions_ref), (image_hbm, image_ref), (shifts_hbm, shifts_ref)), sems
    )
    for copy in copies:
        copy.wait()
    w = weights_at(fractions_ref, 0, 0)
    depth = image_ref.shape[0]
    for layer in range(depth):
        out_ref[layer] = x_pass(image_ref[layer], shifts_ref[0, 0, layer], w)
        low_ref[layer, 0 : PLAN.first, :] = out_ref[layer, 0 : PLAN.first, :]
        high_ref[layer, 0 : PLAN.first, :] = out_ref[layer, HEIGHT - PLAN.first :, :]
        for key, place in PLAN.places.items():
            count = PLAN.halos[key]
            source = shifts_ref.at[key[0], key[1], layer]
            low_ref[layer, place : place + count, :] = source[0:count, :].astype(jnp.float32)
            high_ref[layer, place : place + count, :] = source[HEIGHT - count :, :].astype(jnp.float32)


def y_kernel(step, image_ref, low_ref, high_ref, before_ref, after_ref, shifts_ref, fractions_ref,
             out_ref, padded_ref, filtered_ref, wide_ref):
    rows = out_ref.shape[1]
    w = weights_at(fractions_ref, step, 1)
    depth = image_ref.shape[0]
    halo = PLAN.halos[step, 1] + 3
    for layer in range(depth):
        store_wide(
            padded_ref, layer, low_ref[layer, 0:halo, :], image_ref[layer], high_ref[layer, 0:halo, :]
        )
        moves = PLAN.moves((before_ref, after_ref, shifts_ref), (step, 1), layer, wide_ref)
        out_ref[layer] = y_pass(padded_ref, filtered_ref, layer, rows, moves, w)


def z_x_y_kernel(step, rows_out, below_ref, image_ref, above_ref, before_ref, after_ref, shifts_ref,
                 fractions_ref, *rest):
    *outs, padded_ref, filtered_y_ref, filtered_ref, wide_ref = rest
    refs = (before_ref, after_ref, shifts_ref)
    depth = image_ref.shape[0]
    z_filter(layers_of(below_ref, image_ref, above_ref, 3), filtered_ref, weights_at(fractions_ref, step, 2))
    wx = weights_at(fractions_ref, step + 1, 0)
    wy = weights_at(fractions_ref, step + 1, 1)
    rows = image_ref.shape[1]
    for layer in range(depth):
        moves = PLAN.moves(refs, (step, 2), layer, wide_ref)
        value = choose(moves, [filtered_ref[layer + k] for k in range(4)])
        moves = PLAN.moves(refs, (step + 1, 0), layer, wide_ref)
        value = x_pass(value, moves, wx)
        if rows_out is None:
            outs[0][layer] = value
            outs[1][layer, 0 : PLAN.second, :] = outs[0][layer, 0 : PLAN.second, :]
            outs[2][layer, 0 : PLAN.second, :] = outs[0][layer, HEIGHT - PLAN.second :, :]
            continue
        padded_ref[layer, 0:rows, :] = value
        padded_ref[layer, rows:, :] = jnp.zeros((padded_ref.shape[1] - rows, NX), jnp.float32)
        moves = PLAN.moves(refs, (step + 1, 1), layer, wide_ref.at[:, 0:rows_out, :])
        value = y_pass(padded_ref, filtered_y_ref, layer, rows_out, moves, wy)
        outs[0][layer] = value
        if len(outs) > 1:
            if layer < 3:
                outs[1][layer] = value
            if layer >= depth - 3:
                outs[2][layer - depth + 3] = value
    if len(outs) > 1 and rows_out is not None:
        outs[1][3] = shifts_ref[3, 2, 0].astype(jnp.float32)
        outs[2][3] = shifts_ref[3, 2, depth - 1].astype(jnp.float32)


def split(x):
    high = x.astype(jnp.bfloat16)
    return high, (x - high.astype(jnp.float32)).astype(jnp.bfloat16)


def product(a, b):
    return jnp.dot(a, b, preferred_element_type=jnp.float32)


def force_kernel(below_ref, image_ref, above_ref, before_ref, after_ref, shifts_ref, fractions_ref,
                 first_ref, last_ref, target_ref, table_high_ref, table_low_ref, pairs_ref, ends_ref,
                 out_ref, spectrum_ref, coarse_ref, parcels_ref, filtered_ref, wide_ref, frame_ref, force_ref,
                 tails_ref):
    refs = (before_ref, after_ref, shifts_ref)
    depth = image_ref.shape[0]
    z_filter(layers_of(below_ref, image_ref, above_ref, 4), filtered_ref, weights_at(fractions_ref, 3, 2))
    own = slice(1, 1 + HEIGHT)
    outer = []
    for moves_ref, base in ((first_ref, 0), (last_ref, depth + 1)):
        outer.append(choose(moves_ref[3], [filtered_ref[base + k, own, :] for k in range(4)]))
    for layer in range(depth):
        moves = PLAN.moves(refs, (3, 2), layer, wide_ref)
        frame_ref[layer] = choose(moves, [filtered_ref[layer + 1 + k] for k in range(4)])
    for layer in range(depth):
        image = frame_ref[layer, own, :]
        out_ref[layer] = image
        miss = (image - target_ref[layer]) * 0.5
        below = outer[0] if layer == 0 else frame_ref[layer - 1, own, :]
        above = outer[1] if layer == depth - 1 else frame_ref[layer + 1, own, :]
        slopes = (
            pltpu.roll(image, NX - 1, 1) - pltpu.roll(image, 1, 1),
            frame_ref[layer, 2 : 2 + HEIGHT, :] - frame_ref[layer, 0:HEIGHT, :],
            above - below,
        )
        for way in range(3):
            place = (way * depth + layer) * HEIGHT
            force_ref[place : place + HEIGHT, :] = miss * slopes[way]
    high, low = split(force_ref[...])
    result = product(high, table_high_ref[...])
    result = result + product(high, table_low_ref[...])
    result = result + product(low, table_high_ref[...])
    spectrum_ref[...] = result[:, :NX]
    high, low = split(result[:, NX:])
    coarse = product(pairs_ref[...], high) + product(pairs_ref[...], low)
    coarse_ref[...] = coarse.reshape(coarse_ref.shape)
    across = NX // 128
    for side in range(2):
        for line in range(3 * depth):
            part = spectrum_ref[line * HEIGHT : (line + 1) * HEIGHT, :] * ends_ref[side]
            row = jnp.sum(part, axis=0, keepdims=True)
            place = (side * 3 * depth + line) * across
            for lane in range(across):
                tails_ref[place + lane, :] = row[0, lane * 128 : (lane + 1) * 128]
    for peer in range(parcels_ref.shape[0]):
        parcels_ref[peer] = tails_ref[...]


def load_kernel(*refs):
    count = len(refs) // 2
    for i in range(count):
        refs[count + i][...] = refs[i][...]


def carry_kernel(place_ref, carried_ref, tables_ref, out_ref, sums_ref):
    peers = carried_ref.shape[0]
    across = NX // 128
    lines = out_ref.shape[1]
    rows = lines * across
    place = place_ref[0]
    for side, sign in ((0, -1), (1, 1)):
        total = jnp.zeros((rows, 128), jnp.float32)
        for away in range(peers, 0, -1):
            peer = lax.rem(place + sign * away + peers, peers)
            total = total * tables_ref[0] + carried_ref[peer, side * rows : (side + 1) * rows, :]
        sums_ref[side] = total * tables_ref[1]
        for line in range(lines):
            for lane in range(across):
                out_ref[side, line, lane * 128 : (lane + 1) * 128] = sums_ref[side, line * across + lane, :]


def stencil_kernel(before_ref, own_ref, after_ref, stencil_ref, own_out, up_out, down_out, far_out,
                   up_two_out, down_two_out, wide_ref, part_ref):
    reach = CHEB - 1
    ways, layers, half = own_ref.shape[0], own_ref.shape[1], own_ref.shape[2]
    for way in range(ways):
        for layer in range(layers):
            wide_ref[layer, 0:half, :] = before_ref[way, layer]
            wide_ref[layer, half : 2 * half, :] = own_ref[way, layer]
            wide_ref[layer, 2 * half :, :] = after_ref[way, layer]
            sums = [own_ref[way, layer]]
            for k in range(1, reach + 1):
                sums.append(
                    wide_ref[layer, half - k : 2 * half - k, :] + wide_ref[layer, half + k : 2 * half + k, :]
                )
            for dz in range(reach + 1):
                total = stencil_ref[dz, 0:1, :] * sums[0]
                for dy in range(1, reach + 1 - dz):
                    total = total + stencil_ref[dz, dy : dy + 1, :] * sums[dy]
                part_ref[layer, dz] = total

        def term(z):
            near = [part_ref[layer, abs(z - layer)] for layer in range(layers) if abs(z - layer) <= reach]
            return functools.reduce(lambda a, b: a + b, near)

        for layer in range(layers):
            own_out[way, layer] = term(layer)
            up_out[way, layer] = term(layers + layer)
            down_out[way, layer] = term(layer - layers)
            far_out[way, layer] = term(4 * layers) if layer == 0 else term(1 - 4 * layers)
            for block in range(2):
                up_two_out[way, block * layers + layer] = term((2 + block) * layers + layer)
                down_two_out[way, block * layers + layer] = term(-(2 + block) * layers + layer)


def call(kernel, outs, scratch, *args, smem=(), hbm=(), copies=0, limit=12):
    vmem = pl.BlockSpec(memory_space=pltpu.VMEM)
    spaces = {i: pltpu.SMEM for i in smem} | {i: pltpu.HBM for i in hbm}
    specs = [pl.BlockSpec(memory_space=spaces.get(i, pltpu.VMEM)) for i in range(len(args))]
    shape = lambda dims: jax.ShapeDtypeStruct(dims, jnp.float32)
    scratch = [pltpu.VMEM(dims, jnp.float32) if isinstance(dims, tuple) else dims for dims in scratch]
    if copies:
        scratch.append(pltpu.SemaphoreType.DMA((copies,)))
    return pl.pallas_call(
        kernel,
        out_shape=tuple(shape(dims) if isinstance(dims, tuple) else dims for dims in outs),
        in_specs=specs,
        out_specs=tuple(vmem for _ in outs),
        scratch_shapes=scratch,
        compiler_params=pltpu.CompilerParams(vmem_limit_bytes=limit * 2**20),
    )(*args)


def f32(table):
    return jnp.asarray(table, jnp.float32)


def bf16_pair(table):
    high = np.asarray(table, np.float32).astype(ml_dtypes.bfloat16)
    low = (np.asarray(table, np.float64) - high.astype(np.float64)).astype(ml_dtypes.bfloat16)
    return jnp.asarray(high), jnp.asarray(low)


def dot(a, b):
    return jnp.dot(a, b, precision=HIGH, preferred_element_type=jnp.float32)


def on_device(template, target_image, departure_shifts, departure_fractions):
    depth, height = template.shape[0], template.shape[1]
    peers_y = lax.axis_size("gy")
    length_y = height * peers_y
    shifts, fractions = departure_shifts, departure_fractions
    block = lambda layers, rows: (layers, padded_rows(rows), NX)
    full = (depth, height, NX)

    image, low, high = call(
        start_kernel,
        [full, (depth, PLAN.total, NX), (depth, PLAN.total, NX)],
        [full, pltpu.VMEM(shifts.shape, jnp.int32), pltpu.SMEM(fractions.shape, jnp.float32)],
        template, shifts, fractions, hbm=(0, 1, 2), copies=3, limit=60,
    )
    before = shift_to(high, "gy", 1)
    after = shift_to(low, "gy", -1)
    half, lanes = NX // 2, 128
    across = NX // lanes
    fine_x = hartley(NX)
    coarse_x = np.repeat(hartley(half), 2, axis=0)
    local, ends, spread, ratio, wrap = smoother_tables(length_y, NX, height)
    pair_z = np.kron(np.eye(depth // 2), np.ones((1, 2)))
    pair_y = np.kron(np.eye(height // 2), np.ones((1, 2)))
    pairs = np.kron(np.eye(3), np.kron(pair_z, pair_y))
    tables = (
        target_image,
        *bf16_pair(np.concatenate([fine_x, coarse_x], axis=1)),
        jnp.asarray(pairs / 8.0, jnp.bfloat16),
        f32(ends),
    )
    tables = call(load_kernel, [jax.ShapeDtypeStruct(t.shape, t.dtype) for t in tables], [], *tables)
    halos = (before, after, shifts, fractions)

    def y_step(step, image, low, high):
        rows = padded_rows(height + 2 * PLAN.halos[step, 1])
        (image,) = call(
            functools.partial(y_kernel, step),
            [(depth, rows, NX)],
            [(depth, rows + 8, NX), (depth, rows + 8, NX), (depth, rows, NX)],
            image, low, high, *halos, smem=(6,),
        )
        return image, image[:3], image[depth - 3 :]

    def exchange_z(down, up):
        return shift_to(up, "gz", 1), shift_to(down, "gz", -1)

    def z_step(step, outs, rows_out, below, image, above):
        rows = image.shape[1]
        layers = 3
        return call(
            functools.partial(z_x_y_kernel, step, rows_out),
            outs,
            [(depth, rows + 8, NX), (depth, rows + 8, NX), (depth + 2 * layers - 3, rows, NX), (depth, rows, NX)],
            below, image, above, *halos, smem=(6,),
        )

    image, down, up = y_step(0, image, before, after)
    below, above = exchange_z(down, up)
    image, down, up = z_step(0, [full, full, full], height, below, image, above)
    below, above = exchange_z(down, up)
    outer_low, outer_high = below, above
    edge = (depth, PLAN.second, NX)
    image, low, high = z_step(1, [full, edge, edge], None, below, image, above)
    low, high = shift_to(high, "gy", 1), shift_to(low, "gy", -1)
    image, down, up = y_step(2, image, low, high)
    below, above = exchange_z(down, up)
    rows = padded_rows(height + 2)
    (image,) = z_step(2, [(depth, rows, NX)], rows, below, image, above)
    below, above = exchange_z(image, image)
    below, above, tables = lax.optimization_barrier((below, above, tables))

    lines = 3 * depth
    coarse_shape = (3, depth // 2, height // 2, half)
    image, spectrum, coarse, parcels = call(
        force_kernel,
        [full, (lines * height, NX), coarse_shape, (peers_y, 2 * lines * across, lanes)],
        [
            (3 * depth - 3, rows, NX), (depth, rows, NX), (depth, rows, NX), (lines * height, NX),
            (2 * lines * across, lanes),
        ],
        below, image, above, *halos, outer_low, outer_high, *tables, smem=(6,),
    )

    carried = lax.all_to_all(parcels, "gy", 0, 0, tiled=True)
    beside = shift_to(coarse, "gy", 1), shift_to(coarse, "gy", -1)
    double = (3, depth, height // 2, half)
    own, up, down, far, up_two, down_two = call(
        stencil_kernel,
        [coarse_shape] * 4 + [double] * 2,
        [(depth // 2, 3 * height // 2, half), (depth // 2, CHEB, height // 2, half)],
        beside[0], coarse, beside[1], f32(chebyshev_stencil(half)),
    )
    from_low = shift_to(up_two, "gz", 2)
    from_high = shift_to(down_two, "gz", -2)
    near = depth // 2
    own = own + shift_to(far, "gz", 4) + from_low[:, :near] + from_high[:, :near]
    solved = own + shift_to(up + from_low[:, near:], "gz", 1) + shift_to(down + from_high[:, near:], "gz", -1)

    place = lax.axis_index("gy").reshape(1).astype(jnp.int32)
    weights = f32(np.tile(np.stack([ratio, wrap]).reshape(2, across, lanes), (1, lines, 1)))
    (carries,) = call(
        carry_kernel, [(2, lines, NX)], [(2, lines * across, lanes)], place, carried, weights, smem=(0,)
    )

    spectrum = spectrum.reshape(lines, height, NX)
    smooth = f32(local[0]) * spectrum[:, 0:1]
    for y in range(1, height):
        smooth = smooth + f32(local[y]) * spectrum[:, y : y + 1]
    smooth = smooth + f32(spread[0]) * carries[0][:, None] + f32(spread[1]) * carries[1][:, None]
    smooth = smooth.reshape(lines * height, NX)
    solved = dot(f32(pairs.T), solved.reshape(lines * height // 4, half))
    update = dot(smooth, f32(-fine_x)) + dot(solved, f32(-coarse_x.T))
    return (update.reshape(3, depth, height, NX), image)


def solution(mesh):
    return jax.shard_map(
        on_device,
        mesh=mesh,
        in_specs=(P("gz", "gy", None), P("gz", "gy", None), P(None, None, "gz", "gy", None), P()),
        out_specs=(P(None, "gz", "gy", None), P("gz", "gy", None)),
        check_vma=False,
    )
```

```python
import functools

import jax
import jax.numpy as jnp
import ml_dtypes
import numpy as np
from jax import lax
from jax.experimental import pallas as pl
from jax.experimental.pallas import tpu as pltpu
from jax.sharding import PartitionSpec as P

NX = 512
CHEB = 8
DAMPING = 0.25
ACROSS_WEIGHT = 0.0625
ALONG_SCALE = 32.0
SHIFT = 0.25
HIGH = lax.Precision.HIGH


def hartley(length):
    index = np.arange(length)
    angle = 2.0 * np.pi / length * (np.outer(index, index) % length)
    return (np.cos(angle) + np.sin(angle)) / np.sqrt(length)


def smoother_tables(length_y, length_x, rows):
    weight = (length_y / ALONG_SCALE) ** 2
    sine = np.sin(np.pi * np.arange(length_x) / length_x) ** 2
    a = DAMPING + 4.0 * ACROSS_WEIGHT * sine
    root = np.sqrt(a * a + 4.0 * weight * a)
    r = 2.0 * weight / (a + 2.0 * weight + root)
    y = np.arange(rows)
    local = r ** np.abs(y[:, None, None] - y[None, :, None]) / root
    down = r ** (rows - 1 - y)[:, None]
    up = r ** y[:, None]
    ends = np.stack([down, up])
    spread = np.stack([r ** (y + 1)[:, None], r ** (rows - y)[:, None]]) / root
    return local, ends, spread, r**rows, 1.0 / (1.0 - r**length_y)


def chebyshev_stencil(length_x):
    center = SHIFT + 6.0 - 2.0 * np.cos(2.0 * np.pi * np.arange(length_x) / length_x)
    reach = CHEB - 1
    size = 2 * reach + 1
    rhs = np.zeros((size, size, length_x))
    rhs[reach, reach] = 1.0

    def operate(field):
        wide = np.pad(field, ((1, 1), (1, 1), (0, 0)))
        beside = wide[2:, 1:-1] + wide[:-2, 1:-1] + wide[1:-1, 2:] + wide[1:-1, :-2]
        return center * field - beside

    low = SHIFT
    high = SHIFT + 12.0
    theta = (high + low) / 2.0
    delta = (high - low) / 2.0
    sigma = theta / delta
    ratio_now = 1.0 / sigma
    residual = rhs
    direction = rhs / theta
    result = np.zeros_like(rhs)
    for turn in range(CHEB):
        result = result + direction
        if turn + 1 < CHEB:
            residual = residual - operate(direction)
            ratio_next = 1.0 / (2.0 * sigma - ratio_now)
            direction = ratio_next * ratio_now * direction + 2.0 * ratio_next / delta * residual
            ratio_now = ratio_next
    return result[reach:, reach:]


def ring(axis, offset):
    peers = lax.axis_size(axis)
    return [(i, (i + offset) % peers) for i in range(peers)]


def shift_to(x, axis, offset):
    return lax.ppermute(x, axis, ring(axis, offset))


def cubic_weights(f):
    return (
        -f * (f - 1.0) * (f - 2.0) * (1.0 / 6.0),
        (f + 1.0) * (f - 1.0) * (f - 2.0) * 0.5,
        -(f + 1.0) * f * (f - 2.0) * 0.5,
        (f + 1.0) * f * (f - 1.0) * (1.0 / 6.0),
    )


def blend(w, parts):
    total = w[0] * parts[0]
    for node in range(1, 4):
        total = total + w[node] * parts[node]
    return total


def choose(moves, parts):
    result = parts[3]
    for offset in (0, -1, -2):
        result = jnp.where(moves == offset, parts[offset + 2], result)
    return result


def x_pass(field, moves, w):
    turn = lambda value, by: value if by == 0 else pltpu.roll(value, by % NX, 1)
    filtered = blend(w, [turn(field, 1 - node) for node in range(4)])
    return choose(moves, [turn(filtered, -offset) for offset in (-2, -1, 0, 1)])


LANES = 128
ACROSS = NX // LANES


def lane_part(value, lane):
    return value[:, lane * LANES : (lane + 1) * LANES]


def read_lanes(ref, layer, start, stop):
    return jnp.concatenate([ref[layer, lane, start:stop, :] for lane in range(ACROSS)], axis=1)


def write_lanes(ref, layer, start, value):
    for lane in range(ACROSS):
        ref[layer, lane, start : start + value.shape[0], :] = lane_part(value, lane)


def y_pass(padded_ref, filtered_ref, layer, rows, moves, w):
    results = []
    for lane in range(ACROSS):
        parts = [padded_ref[layer, lane, node : node + rows + 3, :] for node in range(4)]
        filtered_ref[layer, lane, 0 : rows + 3, :] = blend(w, parts)
        parts = [filtered_ref[layer, lane, k : k + rows, :] for k in range(4)]
        results.append(choose(lane_part(moves, lane), parts))
    return jnp.concatenate(results, axis=1)


def z_filter(layers, filtered_ref, w):
    for m in range(len(layers) - 3):
        filtered_ref[m] = blend(w, [layers[m + node]() for node in range(4)])


def layers_of(before_ref, field_ref, after_ref, count):
    return [
        functools.partial(lambda ref, i: ref[i], ref, i)
        for ref, layers in ((before_ref, count), (field_ref, field_ref.shape[0]), (after_ref, count))
        for i in range(layers)
    ]


def weights_at(fractions_ref, step, way):
    return cubic_weights(fractions_ref[step, way])


def padded_rows(count):
    return -(-count // 8) * 8


def store_wide(wide_ref, layer, before, own, after):
    place = 0
    for part in (before, own, after):
        write_lanes(wide_ref, layer, place, part)
        place = place + part.shape[0]
    rest = wide_ref.shape[2] - place
    if rest > 0:
        write_lanes(wide_ref, layer, place, jnp.zeros((rest, NX), wide_ref.dtype))


class Plan:
    def __init__(self, last):
        self.halos = {}
        halo = last
        for step in (3, 2):
            self.halos[step, 2] = self.halos[step, 1] = halo
            halo = halo + 3
            if step == 3:
                self.halos[step, 0] = halo
        self.second = halo
        halo = 0
        for step in (1, 0):
            self.halos[step, 2] = self.halos[step, 1] = halo
            halo = halo + 3
            if step == 1:
                self.halos[step, 0] = halo
        self.first = halo
        self.places = {}
        place = self.first
        for key in sorted(self.halos):
            if self.halos[key] > 0:
                self.places[key] = place
                place = place + self.halos[key]
        self.total = place

    def moves(self, refs, key, layer, wide_ref):
        before_ref, after_ref, shifts_ref = refs
        own = shifts_ref[key[0], key[1], layer]
        if key not in self.places:
            return own
        start, stop = self.places[key], self.places[key] + self.halos[key]
        store_wide(
            wide_ref,
            layer,
            before_ref[layer, start:stop, :],
            own.astype(jnp.float32),
            after_ref[layer, start:stop, :],
        )
        return read_lanes(wide_ref, layer, 0, wide_ref.shape[2])


PLAN = Plan(1)
HEIGHT = 16


def copies_of(pairs, sems):
    copies = [pltpu.make_async_copy(source, place, sems.at[i]) for i, (source, place) in enumerate(pairs)]
    for copy in copies:
        copy.start()
    return copies


def start_kernel(image_hbm, shifts_hbm, fractions_hbm, out_ref, low_ref, high_ref,
                 image_ref, shifts_ref, fractions_ref, sems):
    keys = [(0, 0), *PLAN.places]
    pairs = [(fractions_hbm, fractions_ref), (image_hbm, image_ref)]
    pairs += [(shifts_hbm.at[step, way], shifts_ref.at[step, way]) for step, way in keys]
    copies = copies_of(pairs, sems)
    for copy in copies[:3]:
        copy.wait()
    w = weights_at(fractions_ref, 0, 0)
    depth = image_ref.shape[0]
    for layer in range(depth):
        out_ref[layer] = x_pass(image_ref[layer], shifts_ref[0, 0, layer], w)
    for copy in copies[3:]:
        copy.wait()
    for layer in range(depth):
        low_ref[layer, 0 : PLAN.first, :] = out_ref[layer, 0 : PLAN.first, :]
        high_ref[layer, 0 : PLAN.first, :] = out_ref[layer, HEIGHT - PLAN.first :, :]
        for key, place in PLAN.places.items():
            count = PLAN.halos[key]
            source = shifts_ref.at[key[0], key[1], layer]
            low_ref[layer, place : place + count, :] = source[0:count, :].astype(jnp.float32)
            high_ref[layer, place : place + count, :] = source[HEIGHT - count :, :].astype(jnp.float32)


def y_kernel(step, image_ref, low_ref, high_ref, before_ref, after_ref, shifts_ref, fractions_ref,
             out_ref, padded_ref, filtered_ref, wide_ref):
    rows = out_ref.shape[1]
    w = weights_at(fractions_ref, step, 1)
    depth = image_ref.shape[0]
    halo = PLAN.halos[step, 1] + 3
    for layer in range(depth):
        store_wide(
            padded_ref, layer, low_ref[layer, 0:halo, :], image_ref[layer], high_ref[layer, 0:halo, :]
        )
        moves = PLAN.moves((before_ref, after_ref, shifts_ref), (step, 1), layer, wide_ref)
        out_ref[layer] = y_pass(padded_ref, filtered_ref, layer, rows, moves, w)


def z_x_y_kernel(step, rows_out, below_ref, image_ref, above_ref, before_ref, after_ref, shifts_ref,
                 fractions_ref, *rest):
    *outs, padded_ref, filtered_y_ref, filtered_ref, wide_ref = rest
    refs = (before_ref, after_ref, shifts_ref)
    depth = image_ref.shape[0]
    z_filter(layers_of(below_ref, image_ref, above_ref, 3), filtered_ref, weights_at(fractions_ref, step, 2))
    wx = weights_at(fractions_ref, step + 1, 0)
    wy = weights_at(fractions_ref, step + 1, 1)
    rows = image_ref.shape[1]
    for layer in range(depth):
        moves = PLAN.moves(refs, (step, 2), layer, wide_ref)
        value = choose(moves, [filtered_ref[layer + k] for k in range(4)])
        moves = PLAN.moves(refs, (step + 1, 0), layer, wide_ref)
        value = x_pass(value, moves, wx)
        if rows_out is None:
            outs[0][layer] = value
            outs[1][layer, 0 : PLAN.second, :] = outs[0][layer, 0 : PLAN.second, :]
            outs[2][layer, 0 : PLAN.second, :] = outs[0][layer, HEIGHT - PLAN.second :, :]
            continue
        write_lanes(padded_ref, layer, 0, value)
        write_lanes(padded_ref, layer, rows, jnp.zeros((padded_ref.shape[2] - rows, NX), jnp.float32))
        moves = PLAN.moves(refs, (step + 1, 1), layer, wide_ref.at[:, :, 0:rows_out, :])
        value = y_pass(padded_ref, filtered_y_ref, layer, rows_out, moves, wy)
        outs[0][layer] = value
        if len(outs) > 1:
            if layer < 3:
                outs[1][layer] = value
            if layer >= depth - 3:
                outs[2][layer - depth + 3] = value
    if len(outs) > 1 and rows_out is not None:
        outs[1][3] = shifts_ref[3, 2, 0].astype(jnp.float32)
        outs[2][3] = shifts_ref[3, 2, depth - 1].astype(jnp.float32)


def split(x):
    high = x.astype(jnp.bfloat16)
    return high, (x - high.astype(jnp.float32)).astype(jnp.bfloat16)


def product(a, b):
    return jnp.dot(a, b, preferred_element_type=jnp.float32)


def force_kernel(below_ref, image_ref, above_ref, before_ref, after_ref, shifts_ref, fractions_ref,
                 first_ref, last_ref, target_ref, table_high_ref, table_low_ref, pairs_ref, ends_ref,
                 out_ref, spectrum_ref, coarse_ref, parcels_ref, filtered_ref, wide_ref, frame_ref, force_ref,
                 tails_ref):
    refs = (before_ref, after_ref, shifts_ref)
    depth = image_ref.shape[0]
    z_filter(layers_of(below_ref, image_ref, above_ref, 4), filtered_ref, weights_at(fractions_ref, 3, 2))
    blank = jnp.zeros((1, NX), jnp.float32)
    for layer in range(-1, depth + 1):
        if 0 <= layer < depth:
            moves = PLAN.moves(refs, (3, 2), layer, wide_ref)
        else:
            store_wide(wide_ref, 0, blank, (first_ref if layer < 0 else last_ref)[3], blank)
            moves = read_lanes(wide_ref, 0, 0, wide_ref.shape[2])
        write_lanes(frame_ref, layer + 1, 0, choose(moves, [filtered_ref[layer + 1 + k] for k in range(4)]))
    frames = [read_lanes(frame_ref, layer, 1, 1 + HEIGHT) for layer in range(depth + 2)]
    for layer in range(depth):
        image = frames[layer + 1]
        out_ref[layer] = image
        miss = (image - target_ref[layer]) * 0.5
        slopes = (
            pltpu.roll(image, NX - 1, 1) - pltpu.roll(image, 1, 1),
            read_lanes(frame_ref, layer + 1, 2, 2 + HEIGHT) - read_lanes(frame_ref, layer + 1, 0, HEIGHT),
            frames[layer + 2] - frames[layer],
        )
        for way in range(3):
            place = (way * depth + layer) * HEIGHT
            force_ref[place : place + HEIGHT, :] = miss * slopes[way]
    high, low = split(force_ref[...])
    result = product(high, table_high_ref[...])
    result = result + product(high, table_low_ref[...])
    result = result + product(low, table_high_ref[...])
    spectrum_ref[...] = result[:, :NX]
    high, low = split(result[:, NX:])
    coarse = product(pairs_ref[...], high) + product(pairs_ref[...], low)
    coarse_ref[...] = coarse.reshape(coarse_ref.shape)
    across = NX // 128
    for side in range(2):
        for line in range(3 * depth):
            part = spectrum_ref[line * HEIGHT : (line + 1) * HEIGHT, :] * ends_ref[side]
            row = jnp.sum(part, axis=0, keepdims=True)
            place = (side * 3 * depth + line) * across
            for lane in range(across):
                tails_ref[place + lane, :] = row[0, lane * 128 : (lane + 1) * 128]
    for peer in range(parcels_ref.shape[0]):
        parcels_ref[peer] = tails_ref[...]


def load_kernel(*refs):
    count = len(refs) // 2
    for i in range(count):
        refs[count + i][...] = refs[i][...]


def carry_kernel(place_ref, carried_ref, tables_ref, out_ref, sums_ref):
    peers = carried_ref.shape[0]
    across = NX // 128
    lines = out_ref.shape[1]
    rows = lines * across
    place = place_ref[0]
    for side, sign in ((0, -1), (1, 1)):
        total = jnp.zeros((rows, 128), jnp.float32)
        for away in range(peers, 0, -1):
            peer = lax.rem(place + sign * away + peers, peers)
            total = total * tables_ref[0] + carried_ref[peer, side * rows : (side + 1) * rows, :]
        sums_ref[side] = total * tables_ref[1]
        for line in range(lines):
            for lane in range(across):
                out_ref[side, line, lane * 128 : (lane + 1) * 128] = sums_ref[side, line * across + lane, :]


def stencil_kernel(before_ref, own_ref, after_ref, stencil_ref, own_out, up_out, down_out, far_out,
                   up_two_out, down_two_out, wide_ref, part_ref):
    reach = CHEB - 1
    ways, layers, half = own_ref.shape[0], own_ref.shape[1], own_ref.shape[2]
    for way in range(ways):
        for layer in range(layers):
            wide_ref[layer, 0:half, :] = before_ref[way, layer]
            wide_ref[layer, half : 2 * half, :] = own_ref[way, layer]
            wide_ref[layer, 2 * half :, :] = after_ref[way, layer]
            sums = [own_ref[way, layer]]
            for k in range(1, reach + 1):
                sums.append(
                    wide_ref[layer, half - k : 2 * half - k, :] + wide_ref[layer, half + k : 2 * half + k, :]
                )
            for dz in range(reach + 1):
                total = stencil_ref[dz, 0:1, :] * sums[0]
                for dy in range(1, reach + 1 - dz):
                    total = total + stencil_ref[dz, dy : dy + 1, :] * sums[dy]
                part_ref[layer, dz] = total

        def term(z):
            near = [part_ref[layer, abs(z - layer)] for layer in range(layers) if abs(z - layer) <= reach]
            return functools.reduce(lambda a, b: a + b, near)

        for layer in range(layers):
            own_out[way, layer] = term(layer)
            up_out[way, layer] = term(layers + layer)
            down_out[way, layer] = term(layer - layers)
            far_out[way, layer] = term(4 * layers) if layer == 0 else term(1 - 4 * layers)
            for block in range(2):
                up_two_out[way, block * layers + layer] = term((2 + block) * layers + layer)
                down_two_out[way, block * layers + layer] = term(-(2 + block) * layers + layer)


def call(kernel, outs, scratch, *args, smem=(), hbm=(), copies=0, limit=12):
    vmem = pl.BlockSpec(memory_space=pltpu.VMEM)
    spaces = {i: pltpu.SMEM for i in smem} | {i: pltpu.HBM for i in hbm}
    specs = [pl.BlockSpec(memory_space=spaces.get(i, pltpu.VMEM)) for i in range(len(args))]
    shape = lambda dims: jax.ShapeDtypeStruct(dims, jnp.float32)
    scratch = [pltpu.VMEM(dims, jnp.float32) if isinstance(dims, tuple) else dims for dims in scratch]
    if copies:
        scratch.append(pltpu.SemaphoreType.DMA((copies,)))
    return pl.pallas_call(
        kernel,
        out_shape=tuple(shape(dims) if isinstance(dims, tuple) else dims for dims in outs),
        in_specs=specs,
        out_specs=tuple(vmem for _ in outs),
        scratch_shapes=scratch,
        compiler_params=pltpu.CompilerParams(vmem_limit_bytes=limit * 2**20),
    )(*args)


def f32(table):
    return jnp.asarray(table, jnp.float32)


def bf16_pair(table):
    high = np.asarray(table, np.float32).astype(ml_dtypes.bfloat16)
    low = (np.asarray(table, np.float64) - high.astype(np.float64)).astype(ml_dtypes.bfloat16)
    return jnp.asarray(high), jnp.asarray(low)


def dot(a, b):
    return jnp.dot(a, b, precision=HIGH, preferred_element_type=jnp.float32)


def on_device(template, target_image, departure_shifts, departure_fractions):
    depth, height = template.shape[0], template.shape[1]
    peers_y = lax.axis_size("gy")
    length_y = height * peers_y
    shifts, fractions = departure_shifts, departure_fractions
    block = lambda layers, rows: (layers, padded_rows(rows), NX)
    full = (depth, height, NX)

    image, low, high = call(
        start_kernel,
        [full, (depth, PLAN.total, NX), (depth, PLAN.total, NX)],
        [full, pltpu.VMEM(shifts.shape, jnp.int32), pltpu.SMEM(fractions.shape, jnp.float32)],
        template, shifts, fractions, hbm=(0, 1, 2), copies=3 + len(PLAN.places), limit=60,
    )
    before = shift_to(high, "gy", 1)
    after = shift_to(low, "gy", -1)
    (image,) = call(load_kernel, [jax.ShapeDtypeStruct(full, jnp.float32)], [], image)
    before, after, image = lax.optimization_barrier((before, after, image))
    half, lanes = NX // 2, 128
    across = NX // lanes
    fine_x = hartley(NX)
    coarse_x = np.repeat(hartley(half), 2, axis=0)
    local, ends, spread, ratio, wrap = smoother_tables(length_y, NX, height)
    pair_z = np.kron(np.eye(depth // 2), np.ones((1, 2)))
    pair_y = np.kron(np.eye(height // 2), np.ones((1, 2)))
    pairs = np.kron(np.eye(3), np.kron(pair_z, pair_y))
    tables = (
        target_image,
        *bf16_pair(np.concatenate([fine_x, coarse_x], axis=1)),
        jnp.asarray(pairs / 8.0, jnp.bfloat16),
        f32(ends),
    )
    tables = call(load_kernel, [jax.ShapeDtypeStruct(t.shape, t.dtype) for t in tables], [], *tables)
    halos = (before, after, shifts, fractions)

    def y_step(step, image, low, high):
        rows = padded_rows(height + 2 * PLAN.halos[step, 1])
        (image,) = call(
            functools.partial(y_kernel, step),
            [(depth, rows, NX)],
            [(depth, ACROSS, rows + 8, LANES)] * 2 + [(depth, ACROSS, rows, LANES)],
            image, low, high, *halos, smem=(6,),
        )
        return image, image[:3], image[depth - 3 :]

    def exchange_z(down, up):
        return shift_to(up, "gz", 1), shift_to(down, "gz", -1)

    def z_step(step, outs, rows_out, below, image, above):
        rows = image.shape[1]
        layers = 3
        return call(
            functools.partial(z_x_y_kernel, step, rows_out),
            outs,
            [(depth, ACROSS, rows + 8, LANES)] * 2 + [(depth + 2 * layers - 3, rows, NX), (depth, ACROSS, rows, LANES)],
            below, image, above, *halos, smem=(6,),
        )

    image, down, up = y_step(0, image, before, after)
    below, above = exchange_z(down, up)
    image, down, up = z_step(0, [full, full, full], height, below, image, above)
    below, above = exchange_z(down, up)
    outer_low, outer_high = below, above
    edge = (depth, PLAN.second, NX)
    image, low, high = z_step(1, [full, edge, edge], None, below, image, above)
    low, high = shift_to(high, "gy", 1), shift_to(low, "gy", -1)
    image, down, up = y_step(2, image, low, high)
    below, above = exchange_z(down, up)
    rows = padded_rows(height + 2)
    (image,) = z_step(2, [(depth, rows, NX)], rows, below, image, above)
    below, above = exchange_z(image, image)
    place = lax.axis_index("gy").reshape(1).astype(jnp.int32)
    below, above, tables = lax.optimization_barrier((below, above, tables))

    lines = 3 * depth
    coarse_shape = (3, depth // 2, height // 2, half)
    image, spectrum, coarse, parcels = call(
        force_kernel,
        [full, (lines * height, NX), coarse_shape, (peers_y, 2 * lines * across, lanes)],
        [
            (3 * depth - 3, rows, NX), (depth, ACROSS, rows, LANES), (depth + 2, ACROSS, rows, LANES), (lines * height, NX),
            (2 * lines * across, lanes),
        ],
        below, image, above, *halos, outer_low, outer_high, *tables, smem=(6,),
    )

    carried = lax.all_to_all(parcels, "gy", 0, 0, tiled=True)
    beside = shift_to(coarse, "gy", 1), shift_to(coarse, "gy", -1)
    double = (3, depth, height // 2, half)
    own, up, down, far, up_two, down_two = call(
        stencil_kernel,
        [coarse_shape] * 4 + [double] * 2,
        [(depth // 2, 3 * height // 2, half), (depth // 2, CHEB, height // 2, half)],
        beside[0], coarse, beside[1], f32(chebyshev_stencil(half)),
    )
    own, spectrum, back_x = lax.optimization_barrier((own, spectrum, f32(-fine_x)))
    from_low = shift_to(up_two, "gz", 2)
    from_high = shift_to(down_two, "gz", -2)
    near = depth // 2
    own = own + shift_to(far, "gz", 4) + from_low[:, :near] + from_high[:, :near]
    solved = own + shift_to(up + from_low[:, near:], "gz", 1) + shift_to(down + from_high[:, near:], "gz", -1)

    (back_x,) = call(load_kernel, [jax.ShapeDtypeStruct((NX, NX), jnp.float32)], [], back_x)
    carried, back_x = lax.optimization_barrier((carried, back_x))
    weights = f32(np.tile(np.stack([ratio, wrap]).reshape(2, across, lanes), (1, lines, 1)))
    (carries,) = call(
        carry_kernel, [(2, lines, NX)], [(2, lines * across, lanes)], place, carried, weights, smem=(0,)
    )

    spectrum = spectrum.reshape(lines, height, NX)
    smooth = f32(local[0]) * spectrum[:, 0:1]
    for y in range(1, height):
        smooth = smooth + f32(local[y]) * spectrum[:, y : y + 1]
    smooth = smooth + f32(spread[0]) * carries[0][:, None] + f32(spread[1]) * carries[1][:, None]
    smooth = smooth.reshape(lines * height, NX)
    solved = dot(f32(pairs.T), solved.reshape(lines * height // 4, half))
    update = dot(smooth, back_x) + dot(solved, f32(-coarse_x.T))
    return (update.reshape(3, depth, height, NX), image)


def solution(mesh):
    return jax.shard_map(
        on_device,
        mesh=mesh,
        in_specs=(P("gz", "gy", None), P("gz", "gy", None), P(None, None, "gz", "gy", None), P()),
        out_specs=(P(None, "gz", "gy", None), P("gz", "gy", None)),
        check_vma=False,
    )
```

```python
import functools

import jax
import jax.numpy as jnp
import ml_dtypes
import numpy as np
from jax import lax
from jax.experimental import pallas as pl
from jax.experimental.pallas import tpu as pltpu
from jax.sharding import PartitionSpec as P

NX = 512
CHEB = 8
DAMPING = 0.25
ACROSS_WEIGHT = 0.0625
ALONG_SCALE = 32.0
SHIFT = 0.25
HIGH = lax.Precision.HIGH


def hartley(length):
    index = np.arange(length)
    angle = 2.0 * np.pi / length * (np.outer(index, index) % length)
    return (np.cos(angle) + np.sin(angle)) / np.sqrt(length)


def smoother_tables(length_y, length_x, rows):
    weight = (length_y / ALONG_SCALE) ** 2
    sine = np.sin(np.pi * np.arange(length_x) / length_x) ** 2
    a = DAMPING + 4.0 * ACROSS_WEIGHT * sine
    root = np.sqrt(a * a + 4.0 * weight * a)
    r = 2.0 * weight / (a + 2.0 * weight + root)
    y = np.arange(rows)
    local = r ** np.abs(y[:, None, None] - y[None, :, None]) / root
    down = r ** (rows - 1 - y)[:, None]
    up = r ** y[:, None]
    ends = np.stack([down, up])
    spread = np.stack([r ** (y + 1)[:, None], r ** (rows - y)[:, None]]) / root
    return local, ends, spread, r**rows, 1.0 / (1.0 - r**length_y)


def chebyshev_stencil(length_x):
    center = SHIFT + 6.0 - 2.0 * np.cos(2.0 * np.pi * np.arange(length_x) / length_x)
    reach = CHEB - 1
    size = 2 * reach + 1
    rhs = np.zeros((size, size, length_x))
    rhs[reach, reach] = 1.0

    def operate(field):
        wide = np.pad(field, ((1, 1), (1, 1), (0, 0)))
        beside = wide[2:, 1:-1] + wide[:-2, 1:-1] + wide[1:-1, 2:] + wide[1:-1, :-2]
        return center * field - beside

    low = SHIFT
    high = SHIFT + 12.0
    theta = (high + low) / 2.0
    delta = (high - low) / 2.0
    sigma = theta / delta
    ratio_now = 1.0 / sigma
    residual = rhs
    direction = rhs / theta
    result = np.zeros_like(rhs)
    for turn in range(CHEB):
        result = result + direction
        if turn + 1 < CHEB:
            residual = residual - operate(direction)
            ratio_next = 1.0 / (2.0 * sigma - ratio_now)
            direction = ratio_next * ratio_now * direction + 2.0 * ratio_next / delta * residual
            ratio_now = ratio_next
    return result[reach:, reach:]


def ring(axis, offset):
    peers = lax.axis_size(axis)
    return [(i, (i + offset) % peers) for i in range(peers)]


def shift_to(x, axis, offset):
    return lax.ppermute(x, axis, ring(axis, offset))


def cubic_weights(f):
    return (
        -f * (f - 1.0) * (f - 2.0) * (1.0 / 6.0),
        (f + 1.0) * (f - 1.0) * (f - 2.0) * 0.5,
        -(f + 1.0) * f * (f - 2.0) * 0.5,
        (f + 1.0) * f * (f - 1.0) * (1.0 / 6.0),
    )


def blend(w, parts):
    total = w[0] * parts[0]
    for node in range(1, 4):
        total = total + w[node] * parts[node]
    return total


def choose(moves, parts):
    result = parts[3]
    for offset in (0, -1, -2):
        result = jnp.where(moves == offset, parts[offset + 2], result)
    return result


def x_pass(field, moves, w):
    turn = lambda value, by: value if by == 0 else pltpu.roll(value, by % NX, 1)
    filtered = blend(w, [turn(field, 1 - node) for node in range(4)])
    return choose(moves, [turn(filtered, -offset) for offset in (-2, -1, 0, 1)])


LANES = 128
ACROSS = NX // LANES


def lane_part(value, lane):
    return value[:, lane * LANES : (lane + 1) * LANES]


def read_lanes(ref, layer, start, stop):
    return jnp.concatenate([ref[layer, lane, start:stop, :] for lane in range(ACROSS)], axis=1)


def write_lanes(ref, layer, start, value):
    for lane in range(ACROSS):
        ref[layer, lane, start : start + value.shape[0], :] = lane_part(value, lane)


def y_pass(padded_ref, filtered_ref, layer, rows, moves, w):
    results = []
    for lane in range(ACROSS):
        parts = [padded_ref[layer, lane, node : node + rows + 3, :] for node in range(4)]
        filtered_ref[layer, lane, 0 : rows + 3, :] = blend(w, parts)
        parts = [filtered_ref[layer, lane, k : k + rows, :] for k in range(4)]
        results.append(choose(lane_part(moves, lane), parts))
    return jnp.concatenate(results, axis=1)


def z_filter(layers, filtered_ref, w):
    for m in range(len(layers) - 3):
        filtered_ref[m] = blend(w, [layers[m + node]() for node in range(4)])


def layers_of(before_ref, field_ref, after_ref, count):
    return [
        functools.partial(lambda ref, i: ref[i], ref, i)
        for ref, layers in ((before_ref, count), (field_ref, field_ref.shape[0]), (after_ref, count))
        for i in range(layers)
    ]


def weights_at(fractions_ref, step, way):
    return cubic_weights(fractions_ref[step, way])


def padded_rows(count):
    return -(-count // 8) * 8


def store_wide(wide_ref, layer, before, own, after):
    place = 0
    for part in (before, own, after):
        write_lanes(wide_ref, layer, place, part)
        place = place + part.shape[0]
    rest = wide_ref.shape[2] - place
    if rest > 0:
        write_lanes(wide_ref, layer, place, jnp.zeros((rest, NX), wide_ref.dtype))


class Plan:
    def __init__(self, last):
        self.halos = {}
        halo = last
        for step in (3, 2):
            self.halos[step, 2] = self.halos[step, 1] = halo
            halo = halo + 3
            if step == 3:
                self.halos[step, 0] = halo
        self.second = halo
        halo = 0
        for step in (1, 0):
            self.halos[step, 2] = self.halos[step, 1] = halo
            halo = halo + 3
            if step == 1:
                self.halos[step, 0] = halo
        self.first = halo
        self.places = {}
        place = self.first
        for key in sorted(self.halos):
            if self.halos[key] > 0:
                self.places[key] = place
                place = place + self.halos[key]
        self.total = place

    def moves(self, refs, key, layer, wide_ref):
        before_ref, after_ref, shifts_ref = refs
        own = shifts_ref[key[0], key[1], layer]
        if key not in self.places:
            return own
        start, stop = self.places[key], self.places[key] + self.halos[key]
        store_wide(
            wide_ref,
            layer,
            before_ref[layer, start:stop, :],
            own.astype(jnp.float32),
            after_ref[layer, start:stop, :],
        )
        return read_lanes(wide_ref, layer, 0, wide_ref.shape[2])


PLAN = Plan(1)
HEIGHT = 16


def copies_of(pairs, sems):
    copies = [pltpu.make_async_copy(source, place, sems.at[i]) for i, (source, place) in enumerate(pairs)]
    for copy in copies:
        copy.start()
    return copies


def start_kernel(image_hbm, shifts_hbm, fractions_hbm, out_ref, low_ref, high_ref,
                 image_ref, shifts_ref, fractions_ref, sems):
    keys = [(0, 0), *PLAN.places]
    pairs = [(fractions_hbm, fractions_ref), (image_hbm, image_ref)]
    pairs += [(shifts_hbm.at[step, way], shifts_ref.at[step, way]) for step, way in keys]
    copies = copies_of(pairs, sems)
    for copy in copies[:3]:
        copy.wait()
    w = weights_at(fractions_ref, 0, 0)
    depth = image_ref.shape[0]
    for layer in range(depth):
        out_ref[layer] = x_pass(image_ref[layer], shifts_ref[0, 0, layer], w)
    for copy in copies[3:]:
        copy.wait()
    for layer in range(depth):
        low_ref[layer, 0 : PLAN.first, :] = out_ref[layer, 0 : PLAN.first, :]
        high_ref[layer, 0 : PLAN.first, :] = out_ref[layer, HEIGHT - PLAN.first :, :]
        for key, place in PLAN.places.items():
            count = PLAN.halos[key]
            source = shifts_ref.at[key[0], key[1], layer]
            low_ref[layer, place : place + count, :] = source[0:count, :].astype(jnp.float32)
            high_ref[layer, place : place + count, :] = source[HEIGHT - count :, :].astype(jnp.float32)


def y_kernel(step, image_ref, low_ref, high_ref, before_ref, after_ref, shifts_ref, fractions_ref,
             out_ref, padded_ref, filtered_ref, wide_ref):
    rows = out_ref.shape[1]
    w = weights_at(fractions_ref, step, 1)
    depth = image_ref.shape[0]
    halo = PLAN.halos[step, 1] + 3
    for layer in range(depth):
        store_wide(
            padded_ref, layer, low_ref[layer, 0:halo, :], image_ref[layer], high_ref[layer, 0:halo, :]
        )
        moves = PLAN.moves((before_ref, after_ref, shifts_ref), (step, 1), layer, wide_ref)
        out_ref[layer] = y_pass(padded_ref, filtered_ref, layer, rows, moves, w)


def z_x_y_kernel(step, rows_out, below_ref, image_ref, above_ref, before_ref, after_ref, shifts_ref,
                 fractions_ref, *rest):
    *outs, padded_ref, filtered_y_ref, filtered_ref, wide_ref = rest
    refs = (before_ref, after_ref, shifts_ref)
    depth = image_ref.shape[0]
    z_filter(layers_of(below_ref, image_ref, above_ref, 3), filtered_ref, weights_at(fractions_ref, step, 2))
    wx = weights_at(fractions_ref, step + 1, 0)
    wy = weights_at(fractions_ref, step + 1, 1)
    rows = image_ref.shape[1]
    for layer in range(depth):
        moves = PLAN.moves(refs, (step, 2), layer, wide_ref)
        value = choose(moves, [filtered_ref[layer + k] for k in range(4)])
        moves = PLAN.moves(refs, (step + 1, 0), layer, wide_ref)
        value = x_pass(value, moves, wx)
        if rows_out is None:
            outs[0][layer] = value
            outs[1][layer, 0 : PLAN.second, :] = outs[0][layer, 0 : PLAN.second, :]
            outs[2][layer, 0 : PLAN.second, :] = outs[0][layer, HEIGHT - PLAN.second :, :]
            continue
        write_lanes(padded_ref, layer, 0, value)
        write_lanes(padded_ref, layer, rows, jnp.zeros((padded_ref.shape[2] - rows, NX), jnp.float32))
        moves = PLAN.moves(refs, (step + 1, 1), layer, wide_ref.at[:, :, 0:rows_out, :])
        value = y_pass(padded_ref, filtered_y_ref, layer, rows_out, moves, wy)
        outs[0][layer] = value
        if len(outs) > 1:
            if layer < 3:
                outs[1][layer] = value
            if layer >= depth - 3:
                outs[2][layer - depth + 3] = value
    if len(outs) > 1 and rows_out is not None:
        outs[1][3] = shifts_ref[3, 2, 0].astype(jnp.float32)
        outs[2][3] = shifts_ref[3, 2, depth - 1].astype(jnp.float32)


def split(x):
    high = x.astype(jnp.bfloat16)
    return high, (x - high.astype(jnp.float32)).astype(jnp.bfloat16)


def product(a, b):
    return jnp.dot(a, b, preferred_element_type=jnp.float32)


def force_kernel(below_ref, image_ref, above_ref, before_ref, after_ref, shifts_ref, fractions_ref,
                 first_ref, last_ref, target_ref, table_high_ref, table_low_ref, pairs_ref, ends_ref,
                 out_ref, spectrum_ref, coarse_ref, tails_ref, filtered_ref, wide_ref, frame_ref, force_ref):
    refs = (before_ref, after_ref, shifts_ref)
    depth = image_ref.shape[0]
    z_filter(layers_of(below_ref, image_ref, above_ref, 4), filtered_ref, weights_at(fractions_ref, 3, 2))
    blank = jnp.zeros((1, NX), jnp.float32)
    for layer in range(-1, depth + 1):
        if 0 <= layer < depth:
            moves = PLAN.moves(refs, (3, 2), layer, wide_ref)
        else:
            store_wide(wide_ref, 0, blank, (first_ref if layer < 0 else last_ref)[3], blank)
            moves = read_lanes(wide_ref, 0, 0, wide_ref.shape[2])
        write_lanes(frame_ref, layer + 1, 0, choose(moves, [filtered_ref[layer + 1 + k] for k in range(4)]))
    frames = [read_lanes(frame_ref, layer, 1, 1 + HEIGHT) for layer in range(depth + 2)]
    for layer in range(depth):
        image = frames[layer + 1]
        out_ref[layer] = image
        miss = (image - target_ref[layer]) * 0.5
        slopes = (
            pltpu.roll(image, NX - 1, 1) - pltpu.roll(image, 1, 1),
            read_lanes(frame_ref, layer + 1, 2, 2 + HEIGHT) - read_lanes(frame_ref, layer + 1, 0, HEIGHT),
            frames[layer + 2] - frames[layer],
        )
        for way in range(3):
            place = (way * depth + layer) * HEIGHT
            force_ref[place : place + HEIGHT, :] = miss * slopes[way]
    high, low = split(force_ref[...])
    result = product(high, table_high_ref[...])
    result = result + product(high, table_low_ref[...])
    result = result + product(low, table_high_ref[...])
    spectrum_ref[...] = result[:, :NX]
    high, low = split(result[:, NX:])
    coarse = product(pairs_ref[...], high) + product(pairs_ref[...], low)
    coarse_ref[...] = coarse.reshape(coarse_ref.shape)
    across = NX // 128
    for side in range(2):
        for line in range(3 * depth):
            part = spectrum_ref[line * HEIGHT : (line + 1) * HEIGHT, :] * ends_ref[side]
            row = jnp.sum(part, axis=0, keepdims=True)
            place = (side * 3 * depth + line) * across
            for lane in range(across):
                tails_ref[place + lane, :] = row[0, lane * 128 : (lane + 1) * 128]


def load_kernel(*refs):
    count = len(refs) // 2
    for i in range(count):
        refs[count + i][...] = refs[i][...]


def chip_kernel(place_ref, own_ref, other_ref, tables_ref, out_ref):
    rows = out_ref.shape[1]
    core = lax.rem(place_ref[0], 2)
    for side in range(2):

        @pl.when(core == side)
        def _():
            part = slice(side * rows, (side + 1) * rows)
            value = tables_ref[0] * own_ref[part, :] + other_ref[part, :]
            for peer in range(out_ref.shape[0]):
                out_ref[peer] = value


def carry_kernel(place_ref, carried_ref, other_ref, tables_ref, out_ref, sums_ref):
    chips = carried_ref.shape[0] // 2
    across = NX // 128
    lines = out_ref.shape[1]
    rows = lines * across
    chip = place_ref[0] // 2
    core = lax.rem(place_ref[0], 2)
    ratio = tables_ref[0]
    for side, sign in ((0, -1), (1, 1)):
        total = jnp.zeros((rows, 128), jnp.float32)
        for away in range(chips, 0, -1):
            peer = 2 * lax.rem(chip + sign * away + chips, chips) + side
            total = total * (ratio * ratio) + carried_ref[peer]
        sums_ref[side] = total * tables_ref[1]

        @pl.when(core != side)
        def _():
            sums_ref[side] = other_ref[side * rows : (side + 1) * rows, :] + ratio * sums_ref[side]

        for line in range(lines):
            for lane in range(across):
                out_ref[side, line, lane * 128 : (lane + 1) * 128] = sums_ref[side, line * across + lane, :]


def stencil_kernel(before_ref, own_ref, after_ref, stencil_ref, own_out, up_out, down_out, far_out,
                   up_two_out, down_two_out, wide_ref, part_ref):
    reach = CHEB - 1
    ways, layers, half = own_ref.shape[0], own_ref.shape[1], own_ref.shape[2]
    for way in range(ways):
        for layer in range(layers):
            wide_ref[layer, 0:half, :] = before_ref[way, layer]
            wide_ref[layer, half : 2 * half, :] = own_ref[way, layer]
            wide_ref[layer, 2 * half :, :] = after_ref[way, layer]
            sums = [own_ref[way, layer]]
            for k in range(1, reach + 1):
                sums.append(
                    wide_ref[layer, half - k : 2 * half - k, :] + wide_ref[layer, half + k : 2 * half + k, :]
                )
            for dz in range(reach + 1):
                total = stencil_ref[dz, 0:1, :] * sums[0]
                for dy in range(1, reach + 1 - dz):
                    total = total + stencil_ref[dz, dy : dy + 1, :] * sums[dy]
                part_ref[layer, dz] = total

        def term(z):
            near = [part_ref[layer, abs(z - layer)] for layer in range(layers) if abs(z - layer) <= reach]
            return functools.reduce(lambda a, b: a + b, near)

        for layer in range(layers):
            own_out[way, layer] = term(layer)
            up_out[way, layer] = term(layers + layer)
            down_out[way, layer] = term(layer - layers)
            far_out[way, layer] = term(4 * layers) if layer == 0 else term(1 - 4 * layers)
            for block in range(2):
                up_two_out[way, block * layers + layer] = term((2 + block) * layers + layer)
                down_two_out[way, block * layers + layer] = term(-(2 + block) * layers + layer)


def call(kernel, outs, scratch, *args, smem=(), hbm=(), copies=0, limit=12):
    vmem = pl.BlockSpec(memory_space=pltpu.VMEM)
    spaces = {i: pltpu.SMEM for i in smem} | {i: pltpu.HBM for i in hbm}
    specs = [pl.BlockSpec(memory_space=spaces.get(i, pltpu.VMEM)) for i in range(len(args))]
    shape = lambda dims: jax.ShapeDtypeStruct(dims, jnp.float32)
    scratch = [pltpu.VMEM(dims, jnp.float32) if isinstance(dims, tuple) else dims for dims in scratch]
    if copies:
        scratch.append(pltpu.SemaphoreType.DMA((copies,)))
    return pl.pallas_call(
        kernel,
        out_shape=tuple(shape(dims) if isinstance(dims, tuple) else dims for dims in outs),
        in_specs=specs,
        out_specs=tuple(vmem for _ in outs),
        scratch_shapes=scratch,
        compiler_params=pltpu.CompilerParams(vmem_limit_bytes=limit * 2**20),
    )(*args)


def f32(table):
    return jnp.asarray(table, jnp.float32)


def bf16_pair(table):
    high = np.asarray(table, np.float32).astype(ml_dtypes.bfloat16)
    low = (np.asarray(table, np.float64) - high.astype(np.float64)).astype(ml_dtypes.bfloat16)
    return jnp.asarray(high), jnp.asarray(low)


def dot(a, b):
    return jnp.dot(a, b, precision=HIGH, preferred_element_type=jnp.float32)


def on_device(template, target_image, departure_shifts, departure_fractions):
    depth, height = template.shape[0], template.shape[1]
    peers_y = lax.axis_size("gy")
    length_y = height * peers_y
    shifts, fractions = departure_shifts, departure_fractions
    block = lambda layers, rows: (layers, padded_rows(rows), NX)
    full = (depth, height, NX)

    image, low, high = call(
        start_kernel,
        [full, (depth, PLAN.total, NX), (depth, PLAN.total, NX)],
        [full, pltpu.VMEM(shifts.shape, jnp.int32), pltpu.SMEM(fractions.shape, jnp.float32)],
        template, shifts, fractions, hbm=(0, 1, 2), copies=3 + len(PLAN.places), limit=60,
    )
    before = shift_to(high, "gy", 1)
    after = shift_to(low, "gy", -1)
    (image,) = call(load_kernel, [jax.ShapeDtypeStruct(full, jnp.float32)], [], image)
    before, after, image = lax.optimization_barrier((before, after, image))
    half, lanes = NX // 2, 128
    across = NX // lanes
    fine_x = hartley(NX)
    coarse_x = np.repeat(hartley(half), 2, axis=0)
    local, ends, spread, ratio, wrap = smoother_tables(length_y, NX, height)
    pair_z = np.kron(np.eye(depth // 2), np.ones((1, 2)))
    pair_y = np.kron(np.eye(height // 2), np.ones((1, 2)))
    pairs = np.kron(np.eye(3), np.kron(pair_z, pair_y))
    tables = (
        target_image,
        *bf16_pair(np.concatenate([fine_x, coarse_x], axis=1)),
        jnp.asarray(pairs / 8.0, jnp.bfloat16),
        f32(ends),
    )
    tables = call(load_kernel, [jax.ShapeDtypeStruct(t.shape, t.dtype) for t in tables], [], *tables)
    halos = (before, after, shifts, fractions)

    def y_step(step, image, low, high):
        rows = padded_rows(height + 2 * PLAN.halos[step, 1])
        (image,) = call(
            functools.partial(y_kernel, step),
            [(depth, rows, NX)],
            [(depth, ACROSS, rows + 8, LANES)] * 2 + [(depth, ACROSS, rows, LANES)],
            image, low, high, *halos, smem=(6,),
        )
        return image, image[:3], image[depth - 3 :]

    def exchange_z(down, up):
        return shift_to(up, "gz", 1), shift_to(down, "gz", -1)

    def z_step(step, outs, rows_out, below, image, above):
        rows = image.shape[1]
        layers = 3
        return call(
            functools.partial(z_x_y_kernel, step, rows_out),
            outs,
            [(depth, ACROSS, rows + 8, LANES)] * 2 + [(depth + 2 * layers - 3, rows, NX), (depth, ACROSS, rows, LANES)],
            below, image, above, *halos, smem=(6,),
        )

    image, down, up = y_step(0, image, before, after)
    below, above = exchange_z(down, up)
    image, down, up = z_step(0, [full, full, full], height, below, image, above)
    below, above = exchange_z(down, up)
    outer_low, outer_high = below, above
    edge = (depth, PLAN.second, NX)
    image, low, high = z_step(1, [full, edge, edge], None, below, image, above)
    low, high = shift_to(high, "gy", 1), shift_to(low, "gy", -1)
    image, down, up = y_step(2, image, low, high)
    below, above = exchange_z(down, up)
    rows = padded_rows(height + 2)
    (image,) = z_step(2, [(depth, rows, NX)], rows, below, image, above)
    below, above = exchange_z(image, image)
    place = lax.axis_index("gy").reshape(1).astype(jnp.int32)
    below, above, tables = lax.optimization_barrier((below, above, tables))

    lines = 3 * depth
    coarse_shape = (3, depth // 2, height // 2, half)
    image, spectrum, coarse, tails = call(
        force_kernel,
        [full, (lines * height, NX), coarse_shape, (2 * lines * across, lanes)],
        [
            (3 * depth - 3, rows, NX), (depth, ACROSS, rows, LANES), (depth + 2, ACROSS, rows, LANES), (lines * height, NX),
        ],
        below, image, above, *halos, outer_low, outer_high, *tables, smem=(6,),
    )

    place = lax.axis_index("gy").reshape(1).astype(jnp.int32)
    weights = f32(np.tile(np.stack([ratio, wrap]).reshape(2, across, lanes), (1, lines, 1)))
    other = lax.ppermute(tails, "gy", [(i, i ^ 1) for i in range(peers_y)])
    (parcels,) = call(
        chip_kernel, [(peers_y, lines * across, lanes)], [], place, tails, other, weights, smem=(0,)
    )
    carried = lax.all_to_all(parcels, "gy", 0, 0, tiled=True)
    beside = shift_to(coarse, "gy", 1), shift_to(coarse, "gy", -1)
    double = (3, depth, height // 2, half)
    own, up, down, far, up_two, down_two = call(
        stencil_kernel,
        [coarse_shape] * 4 + [double] * 2,
        [(depth // 2, 3 * height // 2, half), (depth // 2, CHEB, height // 2, half)],
        beside[0], coarse, beside[1], f32(chebyshev_stencil(half)),
    )
    own, spectrum, back_x = lax.optimization_barrier((own, spectrum, f32(-fine_x)))
    from_low = shift_to(up_two, "gz", 2)
    from_high = shift_to(down_two, "gz", -2)
    near = depth // 2
    own = own + shift_to(far, "gz", 4) + from_low[:, :near] + from_high[:, :near]
    solved = own + shift_to(up + from_low[:, near:], "gz", 1) + shift_to(down + from_high[:, near:], "gz", -1)

    (back_x,) = call(load_kernel, [jax.ShapeDtypeStruct((NX, NX), jnp.float32)], [], back_x)
    carried, back_x = lax.optimization_barrier((carried, back_x))
    (carries,) = call(
        carry_kernel, [(2, lines, NX)], [(2, lines * across, lanes)], place, carried, other, weights, smem=(0,)
    )

    spectrum = spectrum.reshape(lines, height, NX)
    smooth = f32(local[0]) * spectrum[:, 0:1]
    for y in range(1, height):
        smooth = smooth + f32(local[y]) * spectrum[:, y : y + 1]
    smooth = smooth + f32(spread[0]) * carries[0][:, None] + f32(spread[1]) * carries[1][:, None]
    smooth = smooth.reshape(lines * height, NX)
    solved = dot(f32(pairs.T), solved.reshape(lines * height // 4, half))
    update = dot(smooth, back_x) + dot(solved, f32(-coarse_x.T))
    return (update.reshape(3, depth, height, NX), image)


def solution(mesh):
    return jax.shard_map(
        on_device,
        mesh=mesh,
        in_specs=(P("gz", "gy", None), P("gz", "gy", None), P(None, None, "gz", "gy", None), P()),
        out_specs=(P(None, "gz", "gy", None), P("gz", "gy", None)),
        check_vma=False,
    )
```

```python
import functools

import jax
import jax.numpy as jnp
import ml_dtypes
import numpy as np
from jax import lax
from jax.experimental import pallas as pl
from jax.experimental.pallas import tpu as pltpu
from jax.sharding import PartitionSpec as P

NX = 512
CHEB = 8
DAMPING = 0.25
ACROSS_WEIGHT = 0.0625
ALONG_SCALE = 32.0
SHIFT = 0.25
HIGH = lax.Precision.HIGH


def hartley(length):
    index = np.arange(length)
    angle = 2.0 * np.pi / length * (np.outer(index, index) % length)
    return (np.cos(angle) + np.sin(angle)) / np.sqrt(length)


def smoother_tables(length_y, length_x, rows):
    weight = (length_y / ALONG_SCALE) ** 2
    sine = np.sin(np.pi * np.arange(length_x) / length_x) ** 2
    a = DAMPING + 4.0 * ACROSS_WEIGHT * sine
    root = np.sqrt(a * a + 4.0 * weight * a)
    r = 2.0 * weight / (a + 2.0 * weight + root)
    y = np.arange(rows)
    local = r ** np.abs(y[:, None, None] - y[None, :, None]) / root
    down = r ** (rows - 1 - y)[:, None]
    up = r ** y[:, None]
    ends = np.stack([down, up])
    spread = np.stack([r ** (y + 1)[:, None], r ** (rows - y)[:, None]]) / root
    return local, ends, spread, r**rows, 1.0 / (1.0 - r**length_y)


def chebyshev_stencil(length_x):
    center = SHIFT + 6.0 - 2.0 * np.cos(2.0 * np.pi * np.arange(length_x) / length_x)
    reach = CHEB - 1
    size = 2 * reach + 1
    rhs = np.zeros((size, size, length_x))
    rhs[reach, reach] = 1.0

    def operate(field):
        wide = np.pad(field, ((1, 1), (1, 1), (0, 0)))
        beside = wide[2:, 1:-1] + wide[:-2, 1:-1] + wide[1:-1, 2:] + wide[1:-1, :-2]
        return center * field - beside

    low = SHIFT
    high = SHIFT + 12.0
    theta = (high + low) / 2.0
    delta = (high - low) / 2.0
    sigma = theta / delta
    ratio_now = 1.0 / sigma
    residual = rhs
    direction = rhs / theta
    result = np.zeros_like(rhs)
    for turn in range(CHEB):
        result = result + direction
        if turn + 1 < CHEB:
            residual = residual - operate(direction)
            ratio_next = 1.0 / (2.0 * sigma - ratio_now)
            direction = ratio_next * ratio_now * direction + 2.0 * ratio_next / delta * residual
            ratio_now = ratio_next
    return result[reach:, reach:]


def ring(axis, offset):
    peers = lax.axis_size(axis)
    return [(i, (i + offset) % peers) for i in range(peers)]


def shift_to(x, axis, offset):
    return lax.ppermute(x, axis, ring(axis, offset))


def cubic_weights(f):
    return (
        -f * (f - 1.0) * (f - 2.0) * (1.0 / 6.0),
        (f + 1.0) * (f - 1.0) * (f - 2.0) * 0.5,
        -(f + 1.0) * f * (f - 2.0) * 0.5,
        (f + 1.0) * f * (f - 1.0) * (1.0 / 6.0),
    )


def blend(w, parts):
    total = w[0] * parts[0]
    for node in range(1, 4):
        total = total + w[node] * parts[node]
    return total


def choose(moves, parts):
    result = parts[3]
    for offset in (0, -1, -2):
        result = jnp.where(moves == offset, parts[offset + 2], result)
    return result


def x_pass(field, moves, w):
    turn = lambda value, by: value if by == 0 else pltpu.roll(value, by % NX, 1)
    filtered = blend(w, [turn(field, 1 - node) for node in range(4)])
    return choose(moves, [turn(filtered, -offset) for offset in (-2, -1, 0, 1)])


LANES = 128
ACROSS = NX // LANES


def lane_part(value, lane):
    return value[:, lane * LANES : (lane + 1) * LANES]


def read_lanes(ref, layer, start, stop):
    return jnp.concatenate([ref[layer, lane, start:stop, :] for lane in range(ACROSS)], axis=1)


def write_lanes(ref, layer, start, value):
    for lane in range(ACROSS):
        ref[layer, lane, start : start + value.shape[0], :] = lane_part(value, lane)


def y_pass(padded_ref, filtered_ref, layer, rows, moves, w):
    results = []
    for lane in range(ACROSS):
        parts = [padded_ref[layer, lane, node : node + rows + 3, :] for node in range(4)]
        filtered_ref[layer, lane, 0 : rows + 3, :] = blend(w, parts)
        parts = [filtered_ref[layer, lane, k : k + rows, :] for k in range(4)]
        results.append(choose(lane_part(moves, lane), parts))
    return jnp.concatenate(results, axis=1)


def z_filter(layers, filtered_ref, w):
    for m in range(len(layers) - 3):
        filtered_ref[m] = blend(w, [layers[m + node]() for node in range(4)])


def layers_of(before_ref, field_ref, after_ref, count):
    return [
        functools.partial(lambda ref, i: ref[i], ref, i)
        for ref, layers in ((before_ref, count), (field_ref, field_ref.shape[0]), (after_ref, count))
        for i in range(layers)
    ]


def weights_at(fractions_ref, step, way):
    return cubic_weights(fractions_ref[step, way])


def padded_rows(count):
    return -(-count // 8) * 8


def store_wide(wide_ref, layer, before, own, after):
    place = 0
    for part in (before, own, after):
        write_lanes(wide_ref, layer, place, part)
        place = place + part.shape[0]
    rest = wide_ref.shape[2] - place
    if rest > 0:
        write_lanes(wide_ref, layer, place, jnp.zeros((rest, NX), wide_ref.dtype))


class Plan:
    def __init__(self, last):
        self.halos = {}
        halo = last
        for step in (3, 2):
            self.halos[step, 2] = self.halos[step, 1] = halo
            halo = halo + 3
            if step == 3:
                self.halos[step, 0] = halo
        self.second = halo
        halo = 0
        for step in (1, 0):
            self.halos[step, 2] = self.halos[step, 1] = halo
            halo = halo + 3
            if step == 1:
                self.halos[step, 0] = halo
        self.first = halo
        self.places = {}
        place = self.first
        for key in sorted(self.halos):
            if self.halos[key] > 0:
                self.places[key] = place
                place = place + self.halos[key]
        self.total = place

    def moves(self, refs, key, layer, wide_ref):
        before_ref, after_ref, shifts_ref = refs
        own = shifts_ref[key[0], key[1], layer]
        if key not in self.places:
            return own
        start, stop = self.places[key], self.places[key] + self.halos[key]
        store_wide(
            wide_ref,
            layer,
            before_ref[layer, start:stop, :],
            own.astype(jnp.float32),
            after_ref[layer, start:stop, :],
        )
        return read_lanes(wide_ref, layer, 0, wide_ref.shape[2])


PLAN = Plan(1)
HEIGHT = 16


def copies_of(pairs, sems):
    copies = [pltpu.make_async_copy(source, place, sems.at[i]) for i, (source, place) in enumerate(pairs)]
    for copy in copies:
        copy.start()
    return copies


def start_kernel(image_hbm, shifts_hbm, fractions_hbm, out_ref, low_ref, high_ref,
                 image_ref, shifts_ref, fractions_ref, sems):
    keys = [(0, 0), *PLAN.places]
    pairs = [(fractions_hbm, fractions_ref), (image_hbm, image_ref)]
    pairs += [(shifts_hbm.at[step, way], shifts_ref.at[step, way]) for step, way in keys]
    copies = copies_of(pairs, sems)
    for copy in copies[:3]:
        copy.wait()
    w = weights_at(fractions_ref, 0, 0)
    depth = image_ref.shape[0]
    for layer in range(depth):
        out_ref[layer] = x_pass(image_ref[layer], shifts_ref[0, 0, layer], w)
    for copy in copies[3:]:
        copy.wait()
    for layer in range(depth):
        low_ref[layer, 0 : PLAN.first, :] = out_ref[layer, 0 : PLAN.first, :]
        high_ref[layer, 0 : PLAN.first, :] = out_ref[layer, HEIGHT - PLAN.first :, :]
        for key, place in PLAN.places.items():
            count = PLAN.halos[key]
            source = shifts_ref.at[key[0], key[1], layer]
            low_ref[layer, place : place + count, :] = source[0:count, :].astype(jnp.float32)
            high_ref[layer, place : place + count, :] = source[HEIGHT - count :, :].astype(jnp.float32)


def y_kernel(step, image_ref, low_ref, high_ref, before_ref, after_ref, shifts_ref, fractions_ref,
             out_ref, padded_ref, filtered_ref, wide_ref):
    rows = out_ref.shape[1]
    w = weights_at(fractions_ref, step, 1)
    depth = image_ref.shape[0]
    halo = PLAN.halos[step, 1] + 3
    for layer in range(depth):
        store_wide(
            padded_ref, layer, low_ref[layer, 0:halo, :], image_ref[layer], high_ref[layer, 0:halo, :]
        )
        moves = PLAN.moves((before_ref, after_ref, shifts_ref), (step, 1), layer, wide_ref)
        out_ref[layer] = y_pass(padded_ref, filtered_ref, layer, rows, moves, w)


def z_x_y_kernel(step, rows_out, below_ref, image_ref, above_ref, before_ref, after_ref, shifts_ref,
                 fractions_ref, *rest):
    *outs, padded_ref, filtered_y_ref, filtered_ref, wide_ref = rest
    refs = (before_ref, after_ref, shifts_ref)
    depth = image_ref.shape[0]
    z_filter(layers_of(below_ref, image_ref, above_ref, 3), filtered_ref, weights_at(fractions_ref, step, 2))
    wx = weights_at(fractions_ref, step + 1, 0)
    wy = weights_at(fractions_ref, step + 1, 1)
    rows = image_ref.shape[1]
    for layer in range(depth):
        moves = PLAN.moves(refs, (step, 2), layer, wide_ref)
        value = choose(moves, [filtered_ref[layer + k] for k in range(4)])
        moves = PLAN.moves(refs, (step + 1, 0), layer, wide_ref)
        value = x_pass(value, moves, wx)
        if rows_out is None:
            outs[0][layer] = value
            outs[1][layer, 0 : PLAN.second, :] = outs[0][layer, 0 : PLAN.second, :]
            outs[2][layer, 0 : PLAN.second, :] = outs[0][layer, HEIGHT - PLAN.second :, :]
            continue
        write_lanes(padded_ref, layer, 0, value)
        write_lanes(padded_ref, layer, rows, jnp.zeros((padded_ref.shape[2] - rows, NX), jnp.float32))
        moves = PLAN.moves(refs, (step + 1, 1), layer, wide_ref.at[:, :, 0:rows_out, :])
        value = y_pass(padded_ref, filtered_y_ref, layer, rows_out, moves, wy)
        outs[0][layer] = value
        if len(outs) > 1:
            if layer < 3:
                outs[1][layer] = value
            if layer >= depth - 3:
                outs[2][layer - depth + 3] = value
    if len(outs) > 1 and rows_out is not None:
        outs[1][3] = shifts_ref[3, 2, 0].astype(jnp.float32)
        outs[2][3] = shifts_ref[3, 2, depth - 1].astype(jnp.float32)


def split(x):
    high = x.astype(jnp.bfloat16)
    return high, (x - high.astype(jnp.float32)).astype(jnp.bfloat16)


def product(a, b):
    return jnp.dot(a, b, preferred_element_type=jnp.float32)


def force_kernel(below_ref, image_ref, above_ref, before_ref, after_ref, shifts_ref, fractions_ref,
                 first_ref, last_ref, target_ref, table_high_ref, table_low_ref, pairs_ref, ends_ref,
                 out_ref, spectrum_ref, coarse_ref, tails_ref, filtered_ref, wide_ref, frame_ref, force_ref):
    refs = (before_ref, after_ref, shifts_ref)
    depth = image_ref.shape[0]
    z_filter(layers_of(below_ref, image_ref, above_ref, 4), filtered_ref, weights_at(fractions_ref, 3, 2))
    blank = jnp.zeros((1, NX), jnp.float32)
    for layer in range(-1, depth + 1):
        if 0 <= layer < depth:
            moves = PLAN.moves(refs, (3, 2), layer, wide_ref)
        else:
            store_wide(wide_ref, 0, blank, (first_ref if layer < 0 else last_ref)[3], blank)
            moves = read_lanes(wide_ref, 0, 0, wide_ref.shape[2])
        write_lanes(frame_ref, layer + 1, 0, choose(moves, [filtered_ref[layer + 1 + k] for k in range(4)]))
    frames = [read_lanes(frame_ref, layer, 1, 1 + HEIGHT) for layer in range(depth + 2)]
    for layer in range(depth):
        image = frames[layer + 1]
        out_ref[layer] = image
        miss = (image - target_ref[layer]) * 0.5
        slopes = (
            pltpu.roll(image, NX - 1, 1) - pltpu.roll(image, 1, 1),
            read_lanes(frame_ref, layer + 1, 2, 2 + HEIGHT) - read_lanes(frame_ref, layer + 1, 0, HEIGHT),
            frames[layer + 2] - frames[layer],
        )
        for way in range(3):
            place = (way * depth + layer) * HEIGHT
            force_ref[place : place + HEIGHT, :] = miss * slopes[way]
    high, low = split(force_ref[...])
    result = product(high, table_high_ref[...])
    result = result + product(high, table_low_ref[...])
    result = result + product(low, table_high_ref[...])
    spectrum_ref[...] = result[:, :NX]
    high, low = split(result[:, NX:])
    coarse = product(pairs_ref[...], high) + product(pairs_ref[...], low)
    coarse_ref[...] = coarse.reshape(coarse_ref.shape)
    across = NX // 128
    for side in range(2):
        for line in range(3 * depth):
            part = spectrum_ref[line * HEIGHT : (line + 1) * HEIGHT, :] * ends_ref[side]
            row = jnp.sum(part, axis=0, keepdims=True)
            place = (side * 3 * depth + line) * across
            for lane in range(across):
                tails_ref[place + lane, :] = row[0, lane * 128 : (lane + 1) * 128]


def load_kernel(*refs):
    count = len(refs) // 2
    for i in range(count):
        refs[count + i][...] = refs[i][...]


def chip_kernel(place_ref, own_ref, other_ref, tables_ref, out_ref):
    rows = out_ref.shape[1]
    core = lax.rem(place_ref[0], 2)
    for side in range(2):

        @pl.when(core == side)
        def _():
            part = slice(side * rows, (side + 1) * rows)
            value = tables_ref[0] * own_ref[part, :] + other_ref[part, :]
            for peer in range(out_ref.shape[0]):
                out_ref[peer] = value


def final_kernel(place_ref, carried_ref, other_ref, tables_ref, smooth_ref, solved_ref, spread_ref, pairs_ref,
                 table_high_ref, table_low_ref, out_ref, sums_ref, carries_ref, joined_ref):
    chips = carried_ref.shape[0] // 2
    across = NX // 128
    lines = carries_ref.shape[1]
    rows = lines * across
    chip = place_ref[0] // 2
    core = lax.rem(place_ref[0], 2)
    ratio = tables_ref[0]
    for side, sign in ((0, -1), (1, 1)):
        total = jnp.zeros((rows, 128), jnp.float32)
        for away in range(chips, 0, -1):
            peer = 2 * lax.rem(chip + sign * away + chips, chips) + side
            total = total * (ratio * ratio) + carried_ref[peer]
        sums_ref[side] = total * tables_ref[1]

        @pl.when(core != side)
        def _():
            sums_ref[side] = other_ref[side * rows : (side + 1) * rows, :] + ratio * sums_ref[side]

        for line in range(lines):
            for lane in range(across):
                carries_ref[side, line, lane * 128 : (lane + 1) * 128] = sums_ref[side, line * across + lane, :]
    for line in range(lines):
        part = slice(line * HEIGHT, (line + 1) * HEIGHT)
        value = smooth_ref[part, :] + spread_ref[0] * carries_ref[0, line : line + 1, :]
        joined_ref[part, 0:NX] = value + spread_ref[1] * carries_ref[1, line : line + 1, :]
    high, low = split(solved_ref[...])
    joined_ref[:, NX:] = product(pairs_ref[...], high) + product(pairs_ref[...], low)
    high, low = split(joined_ref[...])
    result = product(high, table_high_ref[...])
    result = result + product(high, table_low_ref[...])
    out_ref[...] = result + product(low, table_high_ref[...])


def stencil_kernel(before_ref, own_ref, after_ref, stencil_ref, own_out, up_out, down_out, far_out,
                   up_two_out, down_two_out, wide_ref, part_ref):
    reach = CHEB - 1
    ways, layers, half = own_ref.shape[0], own_ref.shape[1], own_ref.shape[2]
    for way in range(ways):
        for layer in range(layers):
            wide_ref[layer, 0:half, :] = before_ref[way, layer]
            wide_ref[layer, half : 2 * half, :] = own_ref[way, layer]
            wide_ref[layer, 2 * half :, :] = after_ref[way, layer]
            sums = [own_ref[way, layer]]
            for k in range(1, reach + 1):
                sums.append(
                    wide_ref[layer, half - k : 2 * half - k, :] + wide_ref[layer, half + k : 2 * half + k, :]
                )
            for dz in range(reach + 1):
                total = stencil_ref[dz, 0:1, :] * sums[0]
                for dy in range(1, reach + 1 - dz):
                    total = total + stencil_ref[dz, dy : dy + 1, :] * sums[dy]
                part_ref[layer, dz] = total

        def term(z):
            near = [part_ref[layer, abs(z - layer)] for layer in range(layers) if abs(z - layer) <= reach]
            return functools.reduce(lambda a, b: a + b, near)

        for layer in range(layers):
            own_out[way, layer] = term(layer)
            up_out[way, layer] = term(layers + layer)
            down_out[way, layer] = term(layer - layers)
            far_out[way, layer] = term(4 * layers) if layer == 0 else term(1 - 4 * layers)
            for block in range(2):
                up_two_out[way, block * layers + layer] = term((2 + block) * layers + layer)
                down_two_out[way, block * layers + layer] = term(-(2 + block) * layers + layer)


def call(kernel, outs, scratch, *args, smem=(), hbm=(), copies=0, limit=12):
    vmem = pl.BlockSpec(memory_space=pltpu.VMEM)
    spaces = {i: pltpu.SMEM for i in smem} | {i: pltpu.HBM for i in hbm}
    specs = [pl.BlockSpec(memory_space=spaces.get(i, pltpu.VMEM)) for i in range(len(args))]
    shape = lambda dims: jax.ShapeDtypeStruct(dims, jnp.float32)
    scratch = [pltpu.VMEM(dims, jnp.float32) if isinstance(dims, tuple) else dims for dims in scratch]
    if copies:
        scratch.append(pltpu.SemaphoreType.DMA((copies,)))
    return pl.pallas_call(
        kernel,
        out_shape=tuple(shape(dims) if isinstance(dims, tuple) else dims for dims in outs),
        in_specs=specs,
        out_specs=tuple(vmem for _ in outs),
        scratch_shapes=scratch,
        compiler_params=pltpu.CompilerParams(vmem_limit_bytes=limit * 2**20),
    )(*args)


def f32(table):
    return jnp.asarray(table, jnp.float32)


def bf16_pair(table):
    high = np.asarray(table, np.float32).astype(ml_dtypes.bfloat16)
    low = (np.asarray(table, np.float64) - high.astype(np.float64)).astype(ml_dtypes.bfloat16)
    return jnp.asarray(high), jnp.asarray(low)


def dot(a, b):
    return jnp.dot(a, b, precision=HIGH, preferred_element_type=jnp.float32)


def on_device(template, target_image, departure_shifts, departure_fractions):
    depth, height = template.shape[0], template.shape[1]
    peers_y = lax.axis_size("gy")
    length_y = height * peers_y
    shifts, fractions = departure_shifts, departure_fractions
    block = lambda layers, rows: (layers, padded_rows(rows), NX)
    full = (depth, height, NX)

    image, low, high = call(
        start_kernel,
        [full, (depth, PLAN.total, NX), (depth, PLAN.total, NX)],
        [full, pltpu.VMEM(shifts.shape, jnp.int32), pltpu.SMEM(fractions.shape, jnp.float32)],
        template, shifts, fractions, hbm=(0, 1, 2), copies=3 + len(PLAN.places), limit=60,
    )
    before = shift_to(high, "gy", 1)
    after = shift_to(low, "gy", -1)
    (image,) = call(load_kernel, [jax.ShapeDtypeStruct(full, jnp.float32)], [], image)
    before, after, image = lax.optimization_barrier((before, after, image))
    half, lanes = NX // 2, 128
    across = NX // lanes
    fine_x = hartley(NX)
    coarse_x = np.repeat(hartley(half), 2, axis=0)
    local, ends, spread, ratio, wrap = smoother_tables(length_y, NX, height)
    pair_z = np.kron(np.eye(depth // 2), np.ones((1, 2)))
    pair_y = np.kron(np.eye(height // 2), np.ones((1, 2)))
    pairs = np.kron(np.eye(3), np.kron(pair_z, pair_y))
    tables = (
        target_image,
        *bf16_pair(np.concatenate([fine_x, coarse_x], axis=1)),
        jnp.asarray(pairs / 8.0, jnp.bfloat16),
        f32(ends),
    )
    tables = call(load_kernel, [jax.ShapeDtypeStruct(t.shape, t.dtype) for t in tables], [], *tables)
    halos = (before, after, shifts, fractions)

    def y_step(step, image, low, high):
        rows = padded_rows(height + 2 * PLAN.halos[step, 1])
        (image,) = call(
            functools.partial(y_kernel, step),
            [(depth, rows, NX)],
            [(depth, ACROSS, rows + 8, LANES)] * 2 + [(depth, ACROSS, rows, LANES)],
            image, low, high, *halos, smem=(6,),
        )
        return image, image[:3], image[depth - 3 :]

    def exchange_z(down, up):
        return shift_to(up, "gz", 1), shift_to(down, "gz", -1)

    def z_step(step, outs, rows_out, below, image, above):
        rows = image.shape[1]
        layers = 3
        return call(
            functools.partial(z_x_y_kernel, step, rows_out),
            outs,
            [(depth, ACROSS, rows + 8, LANES)] * 2 + [(depth + 2 * layers - 3, rows, NX), (depth, ACROSS, rows, LANES)],
            below, image, above, *halos, smem=(6,),
        )

    image, down, up = y_step(0, image, before, after)
    below, above = exchange_z(down, up)
    image, down, up = z_step(0, [full, full, full], height, below, image, above)
    below, above = exchange_z(down, up)
    outer_low, outer_high = below, above
    edge = (depth, PLAN.second, NX)
    image, low, high = z_step(1, [full, edge, edge], None, below, image, above)
    low, high = shift_to(high, "gy", 1), shift_to(low, "gy", -1)
    image, down, up = y_step(2, image, low, high)
    below, above = exchange_z(down, up)
    rows = padded_rows(height + 2)
    (image,) = z_step(2, [(depth, rows, NX)], rows, below, image, above)
    below, above = exchange_z(image, image)
    place = lax.axis_index("gy").reshape(1).astype(jnp.int32)
    below, above, tables = lax.optimization_barrier((below, above, tables))

    lines = 3 * depth
    coarse_shape = (3, depth // 2, height // 2, half)
    image, spectrum, coarse, tails = call(
        force_kernel,
        [full, (lines * height, NX), coarse_shape, (2 * lines * across, lanes)],
        [
            (3 * depth - 3, rows, NX), (depth, ACROSS, rows, LANES), (depth + 2, ACROSS, rows, LANES), (lines * height, NX),
        ],
        below, image, above, *halos, outer_low, outer_high, *tables, smem=(6,),
    )

    place = lax.axis_index("gy").reshape(1).astype(jnp.int32)
    weights = f32(np.tile(np.stack([ratio, wrap]).reshape(2, across, lanes), (1, lines, 1)))
    other = lax.ppermute(tails, "gy", [(i, i ^ 1) for i in range(peers_y)])
    (parcels,) = call(
        chip_kernel, [(peers_y, lines * across, lanes)], [], place, tails, other, weights, smem=(0,)
    )
    beside = shift_to(coarse, "gy", 1), shift_to(coarse, "gy", -1)
    double = (3, depth, height // 2, half)
    own, up, down, far, up_two, down_two = call(
        stencil_kernel,
        [coarse_shape] * 4 + [double] * 2,
        [(depth // 2, 3 * height // 2, half), (depth // 2, CHEB, height // 2, half)],
        beside[0], coarse, beside[1], f32(chebyshev_stencil(half)),
    )
    back = (
        *bf16_pair(np.concatenate([-fine_x, -coarse_x.T], axis=0)),
        jnp.asarray(pairs.T, jnp.bfloat16),
        f32(spread),
    )
    own, spectrum, back = lax.optimization_barrier((own, spectrum, back))
    parcels, up_two, down_two, far = lax.optimization_barrier((parcels, up_two, down_two, far))
    carried = lax.all_to_all(parcels, "gy", 0, 0, tiled=True)
    from_low = shift_to(up_two, "gz", 2)
    from_high = shift_to(down_two, "gz", -2)
    near = depth // 2
    own = own + shift_to(far, "gz", 4) + from_low[:, :near] + from_high[:, :near]
    solved = own + shift_to(up + from_low[:, near:], "gz", 1) + shift_to(down + from_high[:, near:], "gz", -1)

    back = call(load_kernel, [jax.ShapeDtypeStruct(t.shape, t.dtype) for t in back], [], *back)
    carried, back = lax.optimization_barrier((carried, back))

    spectrum = spectrum.reshape(lines, height, NX)
    smooth = f32(local[0]) * spectrum[:, 0:1]
    for y in range(1, height):
        smooth = smooth + f32(local[y]) * spectrum[:, y : y + 1]
    high_x, low_x, repeats, spread = back
    (update,) = call(
        final_kernel,
        [(lines * height, NX)],
        [(2, lines * across, lanes), (2, lines, NX), (lines * height, NX + half)],
        place, carried, other, weights, smooth.reshape(lines * height, NX),
        solved.reshape(lines * height // 4, half), spread, repeats, high_x, low_x, smem=(0,),
    )
    return (update.reshape(3, depth, height, NX), image)


def solution(mesh):
    return jax.shard_map(
        on_device,
        mesh=mesh,
        in_specs=(P("gz", "gy", None), P("gz", "gy", None), P(None, None, "gz", "gy", None), P()),
        out_specs=(P(None, "gz", "gy", None), P("gz", "gy", None)),
        check_vma=False,
    )
```

```python
import functools

import jax
import jax.numpy as jnp
import ml_dtypes
import numpy as np
from jax import lax
from jax.experimental import pallas as pl
from jax.experimental.pallas import tpu as pltpu
from jax.sharding import PartitionSpec as P

NX = 512
CHEB = 8
DAMPING = 0.25
ACROSS_WEIGHT = 0.0625
ALONG_SCALE = 32.0
SHIFT = 0.25
HIGH = lax.Precision.HIGH


def hartley(length):
    index = np.arange(length)
    angle = 2.0 * np.pi / length * (np.outer(index, index) % length)
    return (np.cos(angle) + np.sin(angle)) / np.sqrt(length)


def smoother_tables(length_y, length_x, rows):
    weight = (length_y / ALONG_SCALE) ** 2
    sine = np.sin(np.pi * np.arange(length_x) / length_x) ** 2
    a = DAMPING + 4.0 * ACROSS_WEIGHT * sine
    root = np.sqrt(a * a + 4.0 * weight * a)
    r = 2.0 * weight / (a + 2.0 * weight + root)
    y = np.arange(rows)
    local = r ** np.abs(y[:, None, None] - y[None, :, None]) / root
    down = r ** (rows - 1 - y)[:, None]
    up = r ** y[:, None]
    ends = np.stack([down, up])
    spread = np.stack([r ** (y + 1)[:, None], r ** (rows - y)[:, None]]) / root
    return local, ends, spread, r**rows, 1.0 / (1.0 - r**length_y)


def chebyshev_stencil(length_x):
    center = SHIFT + 6.0 - 2.0 * np.cos(2.0 * np.pi * np.arange(length_x) / length_x)
    reach = CHEB - 1
    size = 2 * reach + 1
    rhs = np.zeros((size, size, length_x))
    rhs[reach, reach] = 1.0

    def operate(field):
        wide = np.pad(field, ((1, 1), (1, 1), (0, 0)))
        beside = wide[2:, 1:-1] + wide[:-2, 1:-1] + wide[1:-1, 2:] + wide[1:-1, :-2]
        return center * field - beside

    low = SHIFT
    high = SHIFT + 12.0
    theta = (high + low) / 2.0
    delta = (high - low) / 2.0
    sigma = theta / delta
    ratio_now = 1.0 / sigma
    residual = rhs
    direction = rhs / theta
    result = np.zeros_like(rhs)
    for turn in range(CHEB):
        result = result + direction
        if turn + 1 < CHEB:
            residual = residual - operate(direction)
            ratio_next = 1.0 / (2.0 * sigma - ratio_now)
            direction = ratio_next * ratio_now * direction + 2.0 * ratio_next / delta * residual
            ratio_now = ratio_next
    return result[reach:, reach:]


def ring(axis, offset):
    peers = lax.axis_size(axis)
    return [(i, (i + offset) % peers) for i in range(peers)]


def shift_to(x, axis, offset):
    return lax.ppermute(x, axis, ring(axis, offset))


def cubic_weights(f):
    return (
        -f * (f - 1.0) * (f - 2.0) * (1.0 / 6.0),
        (f + 1.0) * (f - 1.0) * (f - 2.0) * 0.5,
        -(f + 1.0) * f * (f - 2.0) * 0.5,
        (f + 1.0) * f * (f - 1.0) * (1.0 / 6.0),
    )


def blend(w, parts):
    total = w[0] * parts[0]
    for node in range(1, 4):
        total = total + w[node] * parts[node]
    return total


def choose(moves, parts):
    result = parts[3]
    for offset in (0, -1, -2):
        result = jnp.where(moves == offset, parts[offset + 2], result)
    return result


def x_pass(field, moves, w):
    turn = lambda value, by: value if by == 0 else pltpu.roll(value, by % NX, 1)
    filtered = blend(w, [turn(field, 1 - node) for node in range(4)])
    return choose(moves, [turn(filtered, -offset) for offset in (-2, -1, 0, 1)])


LANES = 128
ACROSS = NX // LANES


def lane_part(value, lane):
    return value[:, lane * LANES : (lane + 1) * LANES]


def read_lanes(ref, layer, start, stop):
    return jnp.concatenate([ref[layer, lane, start:stop, :] for lane in range(ACROSS)], axis=1)


def write_lanes(ref, layer, start, value):
    for lane in range(ACROSS):
        ref[layer, lane, start : start + value.shape[0], :] = lane_part(value, lane)


def y_pass(padded_ref, filtered_ref, layer, rows, moves, w):
    results = []
    for lane in range(ACROSS):
        parts = [padded_ref[layer, lane, node : node + rows + 3, :] for node in range(4)]
        filtered_ref[layer, lane, 0 : rows + 3, :] = blend(w, parts)
        parts = [filtered_ref[layer, lane, k : k + rows, :] for k in range(4)]
        results.append(choose(lane_part(moves, lane), parts))
    return jnp.concatenate(results, axis=1)


def z_filter(layers, filtered_ref, w):
    for m in range(len(layers) - 3):
        filtered_ref[m] = blend(w, [layers[m + node]() for node in range(4)])


def layers_of(before_ref, field_ref, after_ref, count):
    return [
        functools.partial(lambda ref, i: ref[i], ref, i)
        for ref, layers in ((before_ref, count), (field_ref, field_ref.shape[0]), (after_ref, count))
        for i in range(layers)
    ]


def weights_at(fractions_ref, step, way):
    return cubic_weights(fractions_ref[step, way])


def padded_rows(count):
    return -(-count // 8) * 8


def store_wide(wide_ref, layer, before, own, after):
    place = 0
    for part in (before, own, after):
        write_lanes(wide_ref, layer, place, part)
        place = place + part.shape[0]
    rest = wide_ref.shape[2] - place
    if rest > 0:
        write_lanes(wide_ref, layer, place, jnp.zeros((rest, NX), wide_ref.dtype))


class Plan:
    def __init__(self, last):
        self.halos = {}
        halo = last
        for step in (3, 2):
            self.halos[step, 2] = self.halos[step, 1] = halo
            halo = halo + 3
            if step == 3:
                self.halos[step, 0] = halo
        self.second = halo
        halo = 0
        for step in (1, 0):
            self.halos[step, 2] = self.halos[step, 1] = halo
            halo = halo + 3
            if step == 1:
                self.halos[step, 0] = halo
        self.first = halo
        self.places = {}
        place = self.first
        for key in sorted(self.halos):
            if self.halos[key] > 0:
                self.places[key] = place
                place = place + self.halos[key]
        self.total = place

    def moves(self, refs, key, layer, wide_ref):
        before_ref, after_ref, shifts_ref = refs
        own = shifts_ref[key[0], key[1], layer]
        if key not in self.places:
            return own
        start, stop = self.places[key], self.places[key] + self.halos[key]
        store_wide(
            wide_ref,
            layer,
            before_ref[layer, start:stop, :],
            own.astype(jnp.float32),
            after_ref[layer, start:stop, :],
        )
        return read_lanes(wide_ref, layer, 0, wide_ref.shape[2])


PLAN = Plan(1)
HEIGHT = 16


def copies_of(pairs, sems):
    copies = [pltpu.make_async_copy(source, place, sems.at[i]) for i, (source, place) in enumerate(pairs)]
    for copy in copies:
        copy.start()
    return copies


def start_kernel(image_hbm, shifts_hbm, fractions_hbm, out_ref, low_ref, high_ref,
                 image_ref, shifts_ref, fractions_ref, sems):
    keys = [(0, 0), *PLAN.places]
    pairs = [(fractions_hbm, fractions_ref), (image_hbm, image_ref)]
    pairs += [(shifts_hbm.at[step, way], shifts_ref.at[step, way]) for step, way in keys]
    copies = copies_of(pairs, sems)
    for copy in copies[:3]:
        copy.wait()
    w = weights_at(fractions_ref, 0, 0)
    depth = image_ref.shape[0]
    for layer in range(depth):
        out_ref[layer] = x_pass(image_ref[layer], shifts_ref[0, 0, layer], w)
    for copy in copies[3:]:
        copy.wait()
    for layer in range(depth):
        low_ref[layer, 0 : PLAN.first, :] = out_ref[layer, 0 : PLAN.first, :]
        high_ref[layer, 0 : PLAN.first, :] = out_ref[layer, HEIGHT - PLAN.first :, :]
        for key, place in PLAN.places.items():
            count = PLAN.halos[key]
            source = shifts_ref.at[key[0], key[1], layer]
            low_ref[layer, place : place + count, :] = source[0:count, :].astype(jnp.float32)
            high_ref[layer, place : place + count, :] = source[HEIGHT - count :, :].astype(jnp.float32)


def y_kernel(step, image_ref, low_ref, high_ref, before_ref, after_ref, shifts_ref, fractions_ref,
             out_ref, padded_ref, filtered_ref, wide_ref):
    rows = out_ref.shape[1]
    w = weights_at(fractions_ref, step, 1)
    depth = image_ref.shape[0]
    halo = PLAN.halos[step, 1] + 3
    for layer in range(depth):
        store_wide(
            padded_ref, layer, low_ref[layer, 0:halo, :], image_ref[layer], high_ref[layer, 0:halo, :]
        )
        moves = PLAN.moves((before_ref, after_ref, shifts_ref), (step, 1), layer, wide_ref)
        out_ref[layer] = y_pass(padded_ref, filtered_ref, layer, rows, moves, w)


def z_x_y_kernel(step, rows_out, below_ref, image_ref, above_ref, before_ref, after_ref, shifts_ref,
                 fractions_ref, *rest):
    *outs, padded_ref, filtered_y_ref, filtered_ref, wide_ref = rest
    refs = (before_ref, after_ref, shifts_ref)
    depth = image_ref.shape[0]
    z_filter(layers_of(below_ref, image_ref, above_ref, 3), filtered_ref, weights_at(fractions_ref, step, 2))
    wx = weights_at(fractions_ref, step + 1, 0)
    wy = weights_at(fractions_ref, step + 1, 1)
    rows = image_ref.shape[1]
    for layer in range(depth):
        moves = PLAN.moves(refs, (step, 2), layer, wide_ref)
        value = choose(moves, [filtered_ref[layer + k] for k in range(4)])
        moves = PLAN.moves(refs, (step + 1, 0), layer, wide_ref)
        value = x_pass(value, moves, wx)
        if rows_out is None:
            outs[0][layer] = value
            outs[1][layer, 0 : PLAN.second, :] = outs[0][layer, 0 : PLAN.second, :]
            outs[2][layer, 0 : PLAN.second, :] = outs[0][layer, HEIGHT - PLAN.second :, :]
            continue
        write_lanes(padded_ref, layer, 0, value)
        write_lanes(padded_ref, layer, rows, jnp.zeros((padded_ref.shape[2] - rows, NX), jnp.float32))
        moves = PLAN.moves(refs, (step + 1, 1), layer, wide_ref.at[:, :, 0:rows_out, :])
        value = y_pass(padded_ref, filtered_y_ref, layer, rows_out, moves, wy)
        outs[0][layer] = value
        if len(outs) > 1:
            if layer < 3:
                outs[1][layer] = value
            if layer >= depth - 3:
                outs[2][layer - depth + 3] = value
    if len(outs) > 1 and rows_out is not None:
        outs[1][3] = shifts_ref[3, 2, 0].astype(jnp.float32)
        outs[2][3] = shifts_ref[3, 2, depth - 1].astype(jnp.float32)


def split(x):
    high = x.astype(jnp.bfloat16)
    return high, (x - high.astype(jnp.float32)).astype(jnp.bfloat16)


def product(a, b):
    return jnp.dot(a, b, preferred_element_type=jnp.float32)


def force_kernel(below_ref, image_ref, above_ref, before_ref, after_ref, shifts_ref, fractions_ref,
                 first_ref, last_ref, target_ref, table_high_ref, table_low_ref, pairs_ref, ends_ref,
                 out_ref, spectrum_ref, coarse_ref, tails_ref, filtered_ref, wide_ref, frame_ref, force_ref):
    refs = (before_ref, after_ref, shifts_ref)
    depth = image_ref.shape[0]
    z_filter(layers_of(below_ref, image_ref, above_ref, 4), filtered_ref, weights_at(fractions_ref, 3, 2))
    blank = jnp.zeros((1, NX), jnp.float32)
    for layer in range(-1, depth + 1):
        if 0 <= layer < depth:
            moves = PLAN.moves(refs, (3, 2), layer, wide_ref)
        else:
            store_wide(wide_ref, 0, blank, (first_ref if layer < 0 else last_ref)[3], blank)
            moves = read_lanes(wide_ref, 0, 0, wide_ref.shape[2])
        write_lanes(frame_ref, layer + 1, 0, choose(moves, [filtered_ref[layer + 1 + k] for k in range(4)]))
    frames = [read_lanes(frame_ref, layer, 1, 1 + HEIGHT) for layer in range(depth + 2)]
    for layer in range(depth):
        image = frames[layer + 1]
        out_ref[layer] = image
        miss = (image - target_ref[layer]) * 0.5
        slopes = (
            pltpu.roll(image, NX - 1, 1) - pltpu.roll(image, 1, 1),
            read_lanes(frame_ref, layer + 1, 2, 2 + HEIGHT) - read_lanes(frame_ref, layer + 1, 0, HEIGHT),
            frames[layer + 2] - frames[layer],
        )
        for way in range(3):
            place = (way * depth + layer) * HEIGHT
            force_ref[place : place + HEIGHT, :] = miss * slopes[way]
    high, low = split(force_ref[...])
    result = product(high, table_high_ref[...])
    result = result + product(high, table_low_ref[...])
    result = result + product(low, table_high_ref[...])
    spectrum_ref[...] = result[:, :NX]
    high, low = split(result[:, NX:])
    coarse = product(pairs_ref[...], high) + product(pairs_ref[...], low)
    coarse_ref[...] = coarse.reshape(coarse_ref.shape)
    across = NX // 128
    for side in range(2):
        for line in range(3 * depth):
            part = spectrum_ref[line * HEIGHT : (line + 1) * HEIGHT, :] * ends_ref[side]
            row = jnp.sum(part, axis=0, keepdims=True)
            place = (side * 3 * depth + line) * across
            for lane in range(across):
                tails_ref[place + lane, :] = row[0, lane * 128 : (lane + 1) * 128]


def load_kernel(*refs):
    count = len(refs) // 2
    for i in range(count):
        refs[count + i][...] = refs[i][...]


def chip_kernel(place_ref, own_ref, other_ref, tables_ref, out_ref):
    rows = out_ref.shape[1]
    core = lax.rem(place_ref[0], 2)
    for side in range(2):

        @pl.when(core == side)
        def _():
            part = slice(side * rows, (side + 1) * rows)
            value = tables_ref[0] * own_ref[part, :] + other_ref[part, :]
            for peer in range(out_ref.shape[0]):
                out_ref[peer] = value


def carry_kernel(place_ref, carried_ref, other_ref, tables_ref, out_ref, sums_ref):
    chips = carried_ref.shape[0] // 2
    across = NX // 128
    lines = out_ref.shape[1]
    rows = lines * across
    chip = place_ref[0] // 2
    core = lax.rem(place_ref[0], 2)
    ratio = tables_ref[0]
    for side, sign in ((0, -1), (1, 1)):
        total = jnp.zeros((rows, 128), jnp.float32)
        for away in range(chips, 0, -1):
            peer = 2 * lax.rem(chip + sign * away + chips, chips) + side
            total = total * (ratio * ratio) + carried_ref[peer]
        sums_ref[side] = total * tables_ref[1]

        @pl.when(core != side)
        def _():
            sums_ref[side] = other_ref[side * rows : (side + 1) * rows, :] + ratio * sums_ref[side]

        for line in range(lines):
            for lane in range(across):
                out_ref[side, line, lane * 128 : (lane + 1) * 128] = sums_ref[side, line * across + lane, :]


def stencil_kernel(before_ref, own_ref, after_ref, stencil_ref, own_out, up_out, down_out, far_out,
                   up_two_out, down_two_out, wide_ref, part_ref):
    reach = CHEB - 1
    ways, layers, half = own_ref.shape[0], own_ref.shape[1], own_ref.shape[2]
    for way in range(ways):
        for layer in range(layers):
            wide_ref[layer, 0:half, :] = before_ref[way, layer]
            wide_ref[layer, half : 2 * half, :] = own_ref[way, layer]
            wide_ref[layer, 2 * half :, :] = after_ref[way, layer]
            sums = [own_ref[way, layer]]
            for k in range(1, reach + 1):
                sums.append(
                    wide_ref[layer, half - k : 2 * half - k, :] + wide_ref[layer, half + k : 2 * half + k, :]
                )
            for dz in range(reach + 1):
                total = stencil_ref[dz, 0:1, :] * sums[0]
                for dy in range(1, reach + 1 - dz):
                    total = total + stencil_ref[dz, dy : dy + 1, :] * sums[dy]
                part_ref[layer, dz] = total

        def term(z):
            near = [part_ref[layer, abs(z - layer)] for layer in range(layers) if abs(z - layer) <= reach]
            return functools.reduce(lambda a, b: a + b, near)

        for layer in range(layers):
            own_out[way, layer] = term(layer)
            up_out[way, layer] = term(layers + layer)
            down_out[way, layer] = term(layer - layers)
            far_out[way, layer] = term(4 * layers) if layer == 0 else term(1 - 4 * layers)
            for block in range(2):
                up_two_out[way, block * layers + layer] = term((2 + block) * layers + layer)
                down_two_out[way, block * layers + layer] = term(-(2 + block) * layers + layer)


def call(kernel, outs, scratch, *args, smem=(), hbm=(), copies=0, limit=12):
    vmem = pl.BlockSpec(memory_space=pltpu.VMEM)
    spaces = {i: pltpu.SMEM for i in smem} | {i: pltpu.HBM for i in hbm}
    specs = [pl.BlockSpec(memory_space=spaces.get(i, pltpu.VMEM)) for i in range(len(args))]
    shape = lambda dims: jax.ShapeDtypeStruct(dims, jnp.float32)
    scratch = [pltpu.VMEM(dims, jnp.float32) if isinstance(dims, tuple) else dims for dims in scratch]
    if copies:
        scratch.append(pltpu.SemaphoreType.DMA((copies,)))
    return pl.pallas_call(
        kernel,
        out_shape=tuple(shape(dims) if isinstance(dims, tuple) else dims for dims in outs),
        in_specs=specs,
        out_specs=tuple(vmem for _ in outs),
        scratch_shapes=scratch,
        compiler_params=pltpu.CompilerParams(vmem_limit_bytes=limit * 2**20),
    )(*args)


def f32(table):
    return jnp.asarray(table, jnp.float32)


def bf16_pair(table):
    high = np.asarray(table, np.float32).astype(ml_dtypes.bfloat16)
    low = (np.asarray(table, np.float64) - high.astype(np.float64)).astype(ml_dtypes.bfloat16)
    return jnp.asarray(high), jnp.asarray(low)


def dot(a, b):
    return jnp.dot(a, b, precision=HIGH, preferred_element_type=jnp.float32)


def on_device(template, target_image, departure_shifts, departure_fractions):
    depth, height = template.shape[0], template.shape[1]
    peers_y = lax.axis_size("gy")
    length_y = height * peers_y
    shifts, fractions = departure_shifts, departure_fractions
    block = lambda layers, rows: (layers, padded_rows(rows), NX)
    full = (depth, height, NX)

    image, low, high = call(
        start_kernel,
        [full, (depth, PLAN.total, NX), (depth, PLAN.total, NX)],
        [full, pltpu.VMEM(shifts.shape, jnp.int32), pltpu.SMEM(fractions.shape, jnp.float32)],
        template, shifts, fractions, hbm=(0, 1, 2), copies=3 + len(PLAN.places), limit=60,
    )
    before = shift_to(high, "gy", 1)
    after = shift_to(low, "gy", -1)
    (image,) = call(load_kernel, [jax.ShapeDtypeStruct(full, jnp.float32)], [], image)
    before, after, image = lax.optimization_barrier((before, after, image))
    half, lanes = NX // 2, 128
    across = NX // lanes
    fine_x = hartley(NX)
    coarse_x = np.repeat(hartley(half), 2, axis=0)
    local, ends, spread, ratio, wrap = smoother_tables(length_y, NX, height)
    pair_z = np.kron(np.eye(depth // 2), np.ones((1, 2)))
    pair_y = np.kron(np.eye(height // 2), np.ones((1, 2)))
    pairs = np.kron(np.eye(3), np.kron(pair_z, pair_y))
    tables = (
        target_image,
        *bf16_pair(np.concatenate([fine_x, coarse_x], axis=1)),
        jnp.asarray(pairs / 8.0, jnp.bfloat16),
        f32(ends),
    )
    tables = call(load_kernel, [jax.ShapeDtypeStruct(t.shape, t.dtype) for t in tables], [], *tables)
    halos = (before, after, shifts, fractions)

    def y_step(step, image, low, high):
        rows = padded_rows(height + 2 * PLAN.halos[step, 1])
        (image,) = call(
            functools.partial(y_kernel, step),
            [(depth, rows, NX)],
            [(depth, ACROSS, rows + 8, LANES)] * 2 + [(depth, ACROSS, rows, LANES)],
            image, low, high, *halos, smem=(6,),
        )
        return image, image[:3], image[depth - 3 :]

    def exchange_z(down, up):
        return shift_to(up, "gz", 1), shift_to(down, "gz", -1)

    def z_step(step, outs, rows_out, below, image, above):
        rows = image.shape[1]
        layers = 3
        return call(
            functools.partial(z_x_y_kernel, step, rows_out),
            outs,
            [(depth, ACROSS, rows + 8, LANES)] * 2 + [(depth + 2 * layers - 3, rows, NX), (depth, ACROSS, rows, LANES)],
            below, image, above, *halos, smem=(6,),
        )

    image, down, up = y_step(0, image, before, after)
    below, above = exchange_z(down, up)
    image, down, up = z_step(0, [full, full, full], height, below, image, above)
    below, above = exchange_z(down, up)
    outer_low, outer_high = below, above
    edge = (depth, PLAN.second, NX)
    image, low, high = z_step(1, [full, edge, edge], None, below, image, above)
    low, high = shift_to(high, "gy", 1), shift_to(low, "gy", -1)
    image, down, up = y_step(2, image, low, high)
    below, above = exchange_z(down, up)
    rows = padded_rows(height + 2)
    (image,) = z_step(2, [(depth, rows, NX)], rows, below, image, above)
    below, above = exchange_z(image, image)
    place = lax.axis_index("gy").reshape(1).astype(jnp.int32)
    below, above, tables = lax.optimization_barrier((below, above, tables))

    lines = 3 * depth
    coarse_shape = (3, depth // 2, height // 2, half)
    image, spectrum, coarse, tails = call(
        force_kernel,
        [full, (lines * height, NX), coarse_shape, (2 * lines * across, lanes)],
        [
            (3 * depth - 3, rows, NX), (depth, ACROSS, rows, LANES), (depth + 2, ACROSS, rows, LANES), (lines * height, NX),
        ],
        below, image, above, *halos, outer_low, outer_high, *tables, smem=(6,),
    )

    place = lax.axis_index("gy").reshape(1).astype(jnp.int32)
    weights = f32(np.tile(np.stack([ratio, wrap]).reshape(2, across, lanes), (1, lines, 1)))
    other = lax.ppermute(tails, "gy", [(i, i ^ 1) for i in range(peers_y)])
    (parcels,) = call(
        chip_kernel, [(peers_y, lines * across, lanes)], [], place, tails, other, weights, smem=(0,)
    )
    carried = lax.all_to_all(parcels, "gy", 0, 0, tiled=True)
    beside = shift_to(coarse, "gy", 1), shift_to(coarse, "gy", -1)
    double = (3, depth, height // 2, half)
    own, up, down, far, up_two, down_two = call(
        stencil_kernel,
        [coarse_shape] * 4 + [double] * 2,
        [(depth // 2, 3 * height // 2, half), (depth // 2, CHEB, height // 2, half)],
        beside[0], coarse, beside[1], f32(chebyshev_stencil(half)),
    )
    own, back_x = lax.optimization_barrier((own, f32(-fine_x)))
    from_low = shift_to(up_two, "gz", 2)
    from_high = shift_to(down_two, "gz", -2)
    from_low, spectrum = lax.optimization_barrier((from_low, spectrum))
    near = depth // 2
    own = own + shift_to(far, "gz", 4) + from_low[:, :near] + from_high[:, :near]
    solved = own + shift_to(up + from_low[:, near:], "gz", 1) + shift_to(down + from_high[:, near:], "gz", -1)

    (back_x,) = call(load_kernel, [jax.ShapeDtypeStruct((NX, NX), jnp.float32)], [], back_x)
    carried, back_x = lax.optimization_barrier((carried, back_x))
    (carries,) = call(
        carry_kernel, [(2, lines, NX)], [(2, lines * across, lanes)], place, carried, other, weights, smem=(0,)
    )

    spectrum = spectrum.reshape(lines, height, NX)
    smooth = f32(local[0]) * spectrum[:, 0:1]
    for y in range(1, height):
        smooth = smooth + f32(local[y]) * spectrum[:, y : y + 1]
    smooth = smooth + f32(spread[0]) * carries[0][:, None] + f32(spread[1]) * carries[1][:, None]
    smooth = smooth.reshape(lines * height, NX)
    solved = dot(f32(pairs.T), solved.reshape(lines * height // 4, half))
    update = dot(smooth, back_x) + dot(solved, f32(-coarse_x.T))
    return (update.reshape(3, depth, height, NX), image)


def solution(mesh):
    return jax.shard_map(
        on_device,
        mesh=mesh,
        in_specs=(P("gz", "gy", None), P("gz", "gy", None), P(None, None, "gz", "gy", None), P()),
        out_specs=(P(None, "gz", "gy", None), P("gz", "gy", None)),
        check_vma=False,
    )
```
